512 devices in a mesh: dp: 64 (over x, y, core), rows: 8 (over z).
Axes of the slice: x: 4, y: 8, z: 8, core: 2. Of those that a mesh axis runs over, the one named last changes fastest.
Arguments:
- features: bfloat16 [64, 40, 64, 1024], P('dp', 'rows'), may hold values from -6 to 6
- halting_map: int32 [64, 40, 64], P('dp', 'rows'), may hold values from 1 to 23, as said below
- grad_out: bfloat16 [64, 40, 64, 1024], P('dp', 'rows'), may hold values from -16 to 16
- weight_reduce: bfloat16 [256, 1024], replicated, may hold values from -0.1875 to 0.1875
- weight_conv: bfloat16 [256, 2304], replicated, may hold values from -0.125 to 0.125
- weight_expand: bfloat16 [1024, 256], replicated, may hold values from -0.375 to 0.375
Outputs:
- unit_out: bfloat16 [64, 40, 64, 1024], P('dp', 'rows')
- grad_in: bfloat16 [64, 40, 64, 1024], P('dp', 'rows')
- grad_conv: float32 [256, 2304], P('dp')
- grad_expand: float32 [1024, 256], P('dp')
The draws below stay inside these ranges and needn't reach their ends.
Inputs may be any that keep to these rules, and one draw needn't show every extreme that they name: `halting_map`: the number of units still active at each position; its largest value occurs in every sample.
All inputs are finite; a program needn't handle non-finite values.
Results may differ from the reference program's by a relative error of at most 0.034.
The reference program's roundings to bfloat16 on the way (of `hidden_one`, `columns`, `hidden_two`, `gated`, `grad_two` and `grad_one`) count: a program that leaves them out, or rounds other values in their place, can miss the bound.
Values may be sent and summed in bfloat16 or wider, within the bound.
No kernel may reach another device: no remote copies, remote signals or barrier semaphores. Data moves between devices by JAX's collectives and lax.ppermute only.
A program may use at most 64 MiB of HBM per device.

```python
import jax
import jax.numpy as jnp
from jax import lax

C = 1024
F = 256
UNITS = 23
UNIT = 5
IMG_W = 64
SAMPLES = 64
HEIGHT = 40


def draw_halting_map(key, part):
    key = jax.random.fold_in(key, 7)
    key_row, key_col, key_noise = jax.random.split(key, 3)
    centre_row = jax.random.randint(key_row, (SAMPLES, 1, 1), 0, HEIGHT)
    centre_col = jax.random.randint(key_col, (SAMPLES, 1, 1), 0, IMG_W)
    row_ids = jnp.arange(HEIGHT, dtype=jnp.int32)[None, :, None]
    col_ids = jnp.arange(IMG_W, dtype=jnp.int32)[None, None, :]
    distance = jnp.abs(row_ids - centre_row) + jnp.abs(col_ids - centre_col)
    radius = max((HEIGHT + IMG_W) // 4, 1)
    jitter = jax.random.randint(key_noise, (SAMPLES, HEIGHT, IMG_W), 0, 3)
    counts = UNITS - distance * UNITS // radius + jitter
    return jnp.clip(counts, 1, UNITS).astype(jnp.int32)


def spiked(array, own_key, source, target, blocks, factor):
    def block_of(axis_at):
        return (jnp.arange(array.shape[axis_at]) // (array.shape[axis_at] // blocks)).reshape((-1,) + (1,) * (array.ndim - 1 - axis_at))

    first = jax.random.permutation(own_key, blocks)[block_of(target)]
    second = (block_of(target) + blocks // 2) % blocks
    return jnp.where((block_of(source) == first) | (block_of(source) == second), factor * array, array)


def block_levels(key, shape, cuts, low, high):
    factor_of = 1.0
    for position, parts in cuts:
        heights = jax.random.uniform(jax.random.fold_in(jax.random.fold_in(key, 6), position), (parts,), jnp.float32, low / len(cuts), high / len(cuts))
        factor_of = factor_of * jnp.repeat(jnp.exp(heights), shape[position] // parts).reshape((-1,) + (1,) * (len(shape) - 1 - position))
    return factor_of


def scatter_about(key, dims, deviation, bound, cuts=(), kind=jnp.bfloat16):
    array = deviation * jax.random.normal(key, dims, jnp.float32)
    if cuts:
        array = array * block_levels(key, dims, cuts, -0.22, 0.18)
    return jnp.clip(array, -bound, bound).astype(kind)


def noise_with(rng, shape, deviation, most, cuts, heavy, kind=jnp.bfloat16):
    values = deviation * jax.random.normal(rng, shape, jnp.float32)
    if cuts:
        values = values * block_levels(rng, shape, cuts, -0.22, 0.18)
    return jnp.clip(spiked(values, jax.random.fold_in(rng, 3), *heavy), -most, most).astype(kind)


def setup_inputs(seed: int = 0) -> dict:
    splits = jax.random.split(jax.random.key(seed), 7)
    return {
        "features": scatter_about(splits[0], (SAMPLES, HEIGHT, IMG_W, C), 1.0, 6.0, ((0, 64), (1, 8))),
        "halting_map": draw_halting_map(jax.random.fold_in(splits[6], 71), 0),
        "grad_out": noise_with(splits[2], (SAMPLES, HEIGHT, IMG_W, C), 1.0, 16.0, ((0, 64), (1, 8)), (0, 3, 64, 4.0)),
        "weight_reduce": scatter_about(splits[3], (F, C), C ** -0.5, 0.1875),
        "weight_conv": scatter_about(splits[4], (F, 9 * F), (9 * F) ** -0.5, 0.125),
        "weight_expand": scatter_about(splits[5], (C, F), F ** -0.5, 0.375),
    }


def window_columns(padded):
    sample_count, padded_rows, col_count, chan_count = padded.shape
    row_count = padded_rows - 2
    widened = jnp.pad(padded, ((0, 0), (0, 0), (1, 1), (0, 0)))
    pieces = [widened[:, row_off:row_off + row_count, col_off:col_off + col_count, :] for row_off in range(3) for col_off in range(3)]
    return jnp.concatenate(pieces, axis=3).reshape(sample_count * row_count * col_count, 9 * chan_count)


def flipped_kernel(weight_conv):
    width_f = weight_conv.shape[0]
    kernel = weight_conv.reshape(width_f, 3, 3, -1)[:, ::-1, ::-1, :]
    return jnp.transpose(kernel, (1, 2, 0, 3)).reshape(9 * width_f, -1)


def unit_pass(features, halting_map, grad_out, weight_reduce, weight_conv, weight_expand, flipped):
    row_count, col_count, chan_count = features.shape
    positions = row_count * col_count
    flat_in = features.reshape(positions, chan_count)
    active = (halting_map > UNIT).astype(jnp.float32).reshape(positions, 1)
    pre_one = jnp.dot(flat_in, weight_reduce.T, preferred_element_type=jnp.float32)
    hidden_one = jnp.maximum(pre_one, 0.0).astype(jnp.bfloat16)
    padded_one = jnp.pad(hidden_one.reshape(1, row_count, col_count, -1), ((0, 0), (1, 1), (0, 0), (0, 0)))
    columns = window_columns(padded_one)
    pre_two = jnp.dot(columns, weight_conv.T, preferred_element_type=jnp.float32)
    hidden_two = jnp.maximum(pre_two, 0.0).astype(jnp.bfloat16)
    branch = jnp.dot(hidden_two, weight_expand.T, preferred_element_type=jnp.float32)
    unit_out = (flat_in.astype(jnp.float32) + active * branch).astype(jnp.bfloat16)
    upstream = grad_out.reshape(positions, chan_count)
    gated = (active * upstream.astype(jnp.float32)).astype(jnp.bfloat16)
    expand_part = jnp.dot(gated.T, hidden_two, preferred_element_type=jnp.float32)
    back_two = jnp.dot(gated, weight_expand, preferred_element_type=jnp.float32)
    grad_two = jnp.where(pre_two > 0, back_two, 0.0).astype(jnp.bfloat16)
    conv_part = jnp.dot(grad_two.T, columns, preferred_element_type=jnp.float32)
    padded_two = jnp.pad(grad_two.reshape(1, row_count, col_count, -1), ((0, 0), (1, 1), (0, 0), (0, 0)))
    grad_hidden = jnp.dot(window_columns(padded_two), flipped, preferred_element_type=jnp.float32)
    grad_one = jnp.where(pre_one > 0, grad_hidden, 0.0).astype(jnp.bfloat16)
    back_one = jnp.dot(grad_one, weight_reduce, preferred_element_type=jnp.float32)
    grad_in = (upstream.astype(jnp.float32) + back_one).astype(jnp.bfloat16)
    return (unit_out.reshape(row_count, col_count, chan_count), grad_in.reshape(row_count, col_count, chan_count), conv_part, expand_part)


def reference(features, halting_map, grad_out, weight_reduce, weight_conv, weight_expand):
    flipped = flipped_kernel(weight_conv)
    width_f = weight_conv.shape[0]
    chan_count = features.shape[3]

    def stepper(carry, items):
        image, halting, upstream = items
        outputs, grad_image, conv_part, expand_part = unit_pass(image, halting, upstream, weight_reduce, weight_conv, weight_expand, flipped)
        return (carry[0] + conv_part, carry[1] + expand_part), (outputs, grad_image)

    start = (jnp.zeros((width_f, 9 * width_f), jnp.float32), jnp.zeros((chan_count, width_f), jnp.float32))
    totals, stacked = lax.scan(stepper, start, (features, halting_map, grad_out))
    return (stacked[0], stacked[1], totals[0], totals[1])
```

```python
import functools

import jax
import jax.numpy as jnp
from jax import lax
from jax.experimental import pallas as pl
from jax.experimental.pallas import tpu as pltpu
from jax.sharding import PartitionSpec as P

UNIT = 5
BF = jnp.bfloat16
F32 = jnp.float32

NX, NY, NC, NZ = 4, 8, 2, 8
VMEM = pltpu.CompilerParams(vmem_limit_bytes=56 * 1024 * 1024)


def dp_of(x, y, c):
    return (x * NY + y) * NC + c


def swap_core():
    return [(d, d ^ 1) for d in range(NX * NY * NC)]


def step_x(k):
    return [
        (dp_of(x, y, c), dp_of((x + k) % NX, y, c))
        for x in range(NX)
        for y in range(NY)
        for c in range(NC)
    ]


def step_y(k):
    return [
        (dp_of(x, y, c), dp_of(x, (y + k) % NY, c))
        for x in range(NX)
        for y in range(NY)
        for c in range(NC)
    ]


def step_z(k):
    return [(z, (z + k) % NZ) for z in range(NZ)]


def dot(left, right, left_dim, right_dim):
    return lax.dot_general(
        left, right, (((left_dim,), (right_dim,)), ((), ())), preferred_element_type=F32
    )


def active_column(halting):
    rows, cols = halting.shape
    active = (halting > UNIT).astype(F32)
    at_row = lax.broadcasted_iota(jnp.int32, (cols, cols), 0)
    at_col = lax.broadcasted_iota(jnp.int32, (cols, cols), 1)
    parts = [
        jnp.sum(jnp.where(at_row == at_col, active[r : r + 1, :], 0.0), axis=1, keepdims=True)
        for r in range(rows)
    ]
    return jnp.concatenate(parts, axis=0)


def neighbours(cells, cols):
    count = cells.shape[0]
    wide = cells.astype(F32)
    col = lax.rem(lax.broadcasted_iota(jnp.int32, (count, 1), 0), cols)
    left = jnp.where(col == 0, 0.0, pltpu.roll(wide, 1, 0))
    right = jnp.where(col == cols - 1, 0.0, pltpu.roll(wide, count - 1, 0))
    return left.astype(BF), right.astype(BF)


def enter_kernel(
    halt_ref, feat_ref, grad_ref, reduce_ref, expand_ref,
    hidden_ref, sign_ref, back_ref, up_ref, down_ref,
):
    cols = halt_ref.shape[2]
    rows = halt_ref.shape[1]
    pre_one = dot(feat_ref[...], reduce_ref[...], 1, 1)
    hidden = jnp.maximum(pre_one, 0.0).astype(BF)
    hidden_ref[...] = hidden
    sign_ref[...] = (pre_one > 0).astype(F32).astype(BF)
    back = (active_column(halt_ref[0]) * dot(grad_ref[...], expand_ref[...], 1, 0)).astype(BF)
    back_ref[...] = back
    up_ref[0 : 2 * cols, :] = hidden[0 : 2 * cols]
    up_ref[2 * cols :, :] = back[0:cols]
    down_ref[0 : 2 * cols, :] = hidden[(rows - 2) * cols :]
    down_ref[2 * cols :, :] = back[(rows - 1) * cols :]


def middle_kernel(
    halt_ref, hidden_ref, back_ref, prev_ref, next_ref, grad_ref, conv_ref,
    keep_ref, send_ref, two_ref, gtwo_ref, columns_ref,
):
    rows, cols = halt_ref.shape[1:]
    own = rows * cols
    width = hidden_ref.shape[1]
    place = lax.axis_index("dp")
    my_x, my_y, my_c = place // (NY * NC), (place // NC) % NY, place % NC

    padded = jnp.concatenate([prev_ref[0 : 2 * cols], hidden_ref[...], next_ref[0 : 2 * cols]], axis=0)
    left, right = neighbours(padded, cols)
    wide = own + 2 * cols
    for a in range(3):
        for b, shifted in enumerate((left, padded, right)):
            tap = 3 * a + b
            columns_ref[:, tap * width : (tap + 1) * width] = shifted[a * cols : a * cols + wide]
    pre_two = dot(columns_ref[...], conv_ref[...], 1, 1)
    back = jnp.concatenate([prev_ref[2 * cols :], back_ref[...], next_ref[2 * cols :]], axis=0)
    grad_two = jnp.where(pre_two > 0, back.astype(F32), 0.0).astype(BF)
    gtwo_ref[...] = grad_two
    active = active_column(halt_ref[0])
    hidden_two = (active * jnp.maximum(pre_two[cols : cols + own], 0.0)).astype(BF)
    two_ref[...] = hidden_two

    shape = (width, width)
    at = lax.broadcasted_iota(jnp.int32, shape, 0)
    per_dp = width // (NX * NY * NC)
    j, y = at % per_dp, (at // per_dp) % NY
    x, c = (at // (per_dp * NY)) % NX, at // (per_dp * NY * NX)
    x, y, c = (x + my_x) % NX, (y + my_y) % NY, (c + my_c) % NC
    wanted = dp_of(x, y, c) * per_dp + j
    shuffle = (lax.broadcasted_iota(jnp.int32, shape, 1) == wanted).astype(F32).astype(BF)
    grad_rows = dot(shuffle, grad_two[cols : cols + own], 1, 1).astype(BF)
    conv_part = dot(grad_rows, columns_ref[cols : cols + own, :], 1, 0).astype(BF)
    block = per_dp * NY
    taps = conv_part.shape[1] // width
    for tap in range(taps):
        for rel in range(NX):
            rows_at = slice(tap * block, (tap + 1) * block)
            lanes = slice(tap * width, (tap + 1) * width)
            keep_ref[rel, rows_at, :] = conv_part[rel * block : (rel + 1) * block, lanes]
            send_ref[rel, rows_at, :] = conv_part[(NX + rel) * block : (NX + rel + 1) * block, lanes]
    expand_part = dot(grad_ref[...], hidden_two, 0, 0).astype(BF)
    start = taps * block
    per_dp = expand_part.shape[0] // (NX * NY * NC)
    for x in range(NX):
        rel_x = (x - my_x + NX) % NX
        for y in range(NY):
            at = pl.multiple_of(start + (y - my_y + NY) % NY * per_dp, per_dp)
            first = dp_of(x, y, 0) * per_dp
            zero, one = (expand_part[first + i * per_dp : first + (i + 1) * per_dp] for i in (0, 1))
            keep_ref[rel_x, pl.ds(at, per_dp), :] = jnp.where(my_c == 0, zero, one)
            send_ref[rel_x, pl.ds(at, per_dp), :] = jnp.where(my_c == 0, one, zero)


def leave_kernel(
    feat_ref, grad_ref, two_ref, gtwo_ref, sign_ref, reduce_ref, conv_ref, expand_ref,
    out_ref, gin_ref, columns_ref, stacked_ref, *, cols,
):
    own = feat_ref.shape[0]
    width = two_ref.shape[1]
    out_ref[...] = (feat_ref[...].astype(F32) + dot(two_ref[...], expand_ref[...], 1, 1)).astype(BF)
    grad_two = gtwo_ref[...]
    left, right = neighbours(grad_two, cols)
    for a in range(3):
        for b, shifted in enumerate((right, grad_two, left)):
            tap = 3 * a + b
            at = slice(tap * width, (tap + 1) * width)
            columns_ref[:, at] = shifted[(2 - a) * cols : (2 - a) * cols + own]
            stacked_ref[at, :] = conv_ref[:, at]
    grad_hidden = dot(columns_ref[...], stacked_ref[...], 1, 0)
    grad_one = (grad_hidden * sign_ref[...].astype(F32)).astype(BF)
    gin_ref[...] = (grad_ref[...].astype(F32) + dot(grad_one, reduce_ref[...], 1, 0)).astype(BF)


def core_kernel(keep_ref, got_ref, own_ref, *send_refs):
    total = keep_ref[...].astype(F32) + got_ref[...].astype(F32)
    own_ref[...] = total[0].astype(own_ref.dtype)
    for k, ref in enumerate(send_refs):
        ref[...] = total[k + 1].astype(BF)


def x_kernel(own_ref, *refs):
    got, out = refs[: NX - 1], refs[NX - 1 :]
    total = own_ref[...].astype(F32)
    for ref in got:
        total = total + ref[...].astype(F32)
    rows_conv, rows_expand, taps = 4, 16, 9
    block = rows_conv * NY
    for y, ref in enumerate(out):
        parts = [
            total[tap * block + y * rows_conv : tap * block + (y + 1) * rows_conv] for tap in range(taps)
        ]
        start = taps * block + y * rows_expand
        parts.append(total[start : start + rows_expand])
        ref[...] = jnp.concatenate(parts, axis=0).astype(ref.dtype)


def y_kernel(own_ref, *refs):
    got, out_ref = refs[:-1], refs[-1]
    total = own_ref[...].astype(F32)
    for ref in got:
        total = total + ref[...].astype(F32)
    out_ref[...] = total.astype(out_ref.dtype)


def z_kernel(own_ref, *refs):
    got, (conv_ref, expand_ref) = refs[:-2], refs[-2:]
    total = own_ref[...].astype(F32)
    for ref in got:
        total = total + ref[...].astype(F32)
    rows_conv, width = conv_ref.shape[0], expand_ref.shape[1]
    taps = conv_ref.shape[1] // width
    for tap in range(taps):
        conv_ref[:, tap * width : (tap + 1) * width] = total[tap * rows_conv : (tap + 1) * rows_conv]
    expand_ref[...] = total[taps * rows_conv :]


def call(kernel, outs, *args, scratch=()):
    return pl.pallas_call(
        kernel,
        out_shape=[jax.ShapeDtypeStruct(shape, dtype) for shape, dtype in outs],
        scratch_shapes=list(scratch),
        compiler_params=VMEM,
    )(*args)


def local(features, halting_map, grad_out, weight_reduce, weight_conv, weight_expand):
    samples, rows, cols, chans = features.shape
    width = weight_reduce.shape[0]
    own = samples * rows * cols
    flat_in = features.reshape(own, chans)
    upstream = grad_out.reshape(own, chans)

    hidden, sign, back, up, down = call(
        enter_kernel,
        [((own, width), BF)] * 3 + [((3 * cols, width), BF)] * 2,
        halting_map, flat_in, upstream, weight_reduce, weight_expand,
    )
    from_prev = lax.ppermute(down, "rows", [(i, i + 1) for i in range(NZ - 1)])
    from_next = lax.ppermute(up, "rows", [(i + 1, i) for i in range(NZ - 1)])

    shard = (4 * weight_conv.shape[1] + 16 * width) // width
    part = (NX, NY * shard, width)
    wide = own + 2 * cols
    keep, send, two, gtwo = call(
        middle_kernel,
        [(part, BF), (part, BF), ((own, width), BF), ((wide, width), BF)],
        halting_map, hidden, back, from_prev, from_next, upstream, weight_conv,
        scratch=[pltpu.VMEM((wide, weight_conv.shape[1]), BF)],
    )

    got = lax.ppermute(send, "dp", swap_core())
    out, grad_in = call(
        functools.partial(leave_kernel, cols=cols),
        [((own, chans), BF)] * 2,
        flat_in, upstream, two, gtwo, sign, weight_reduce, weight_conv, weight_expand,
        scratch=[
            pltpu.VMEM((own, weight_conv.shape[1]), BF),
            pltpu.VMEM((weight_conv.shape[1], width), BF),
        ],
    )
    own_x, *sends = call(core_kernel, [(part[1:], F32)] + [(part[1:], BF)] * (NX - 1), keep, got)
    gots = [lax.ppermute(s, "dp", step_x(k + 1)) for k, s in enumerate(sends)]
    small = (shard, width)
    own_y, *sends = call(x_kernel, [(small, F32)] + [(small, BF)] * (NY - 1), own_x, *gots)
    gots = [lax.ppermute(s, "dp", step_y(k + 1)) for k, s in enumerate(sends)]
    (mine,) = call(y_kernel, [(small, F32)], own_y, *gots)
    gots = [lax.ppermute(mine, "rows", step_z(k)) for k in range(1, NZ)]
    grad_conv, grad_expand = call(
        z_kernel, [((4, weight_conv.shape[1]), F32), ((16, width), F32)], mine, *gots
    )
    return (out.reshape(features.shape), grad_in.reshape(features.shape), grad_conv, grad_expand)


def solution(mesh):
    in_specs = (
        P("dp", "rows", None, None),
        P("dp", "rows", None),
        P("dp", "rows", None, None),
        P(),
        P(),
        P(),
    )
    out_specs = (
        P("dp", "rows", None, None),
        P("dp", "rows", None, None),
        P("dp", None),
        P("dp", None),
    )
    return jax.shard_map(local, mesh=mesh, in_specs=in_specs, out_specs=out_specs, check_vma=False)
```

```python
import functools

import jax
import jax.numpy as jnp
from jax import lax
from jax.experimental import pallas as pl
from jax.experimental.pallas import tpu as pltpu
from jax.sharding import Mesh, PartitionSpec as P

UNIT = 5
BF = jnp.bfloat16
F32 = jnp.float32

AXES = ("x", "y_hi", "y_lo", "core", "rows")
NX, NH, NL, NC, NZ = SIZES = (4, 4, 2, 2, 8)
DP = AXES[:4]
VMEM_LIMIT = pltpu.CompilerParams(vmem_limit_bytes=56 * 1024 * 1024)


def dp_of(x, hi, lo, core):
    return ((x * NH + hi) * NL + lo) * NC + core


def dot(left, right, left_dim, right_dim):
    return lax.dot_general(
        left, right, (((left_dim,), (right_dim,)), ((), ())), preferred_element_type=F32
    )


def active_column(halt_ref):
    rows, _, cols = halt_ref.shape
    at_row = lax.broadcasted_iota(jnp.int32, (cols, cols), 0)
    at_col = lax.broadcasted_iota(jnp.int32, (cols, cols), 1)
    parts = [
        jnp.sum(
            jnp.where((at_row == at_col) & (halt_ref[r] > UNIT), 1.0, 0.0), axis=1, keepdims=True
        )
        for r in range(rows)
    ]
    return jnp.concatenate(parts, axis=0)


def neighbours(cells, cols):
    count = cells.shape[0]
    wide = cells.astype(F32)
    col = lax.rem(lax.broadcasted_iota(jnp.int32, (count, 1), 0), cols)
    left = jnp.where(col == 0, 0.0, pltpu.roll(wide, 1, 0))
    right = jnp.where(col == cols - 1, 0.0, pltpu.roll(wide, count - 1, 0))
    return left.astype(BF), right.astype(BF)


def enter_kernel(
    halt_ref, feat_ref, grad_ref, reduce_ref, expand_ref,
    hidden_ref, sign_ref, back_ref, up_ref, down_ref,
):
    rows, _, cols = halt_ref.shape
    pre_one = dot(feat_ref[...], reduce_ref[...], 1, 1)
    hidden = jnp.maximum(pre_one, 0.0).astype(BF)
    hidden_ref[...] = hidden
    sign_ref[...] = (pre_one > 0).astype(F32).astype(BF)
    back = (active_column(halt_ref) * dot(grad_ref[...], expand_ref[...], 1, 0)).astype(BF)
    back_ref[...] = back
    up_ref[0 : 2 * cols, :] = hidden[0 : 2 * cols]
    up_ref[2 * cols :, :] = back[0:cols]
    down_ref[0 : 2 * cols, :] = hidden[(rows - 2) * cols :]
    down_ref[2 * cols :, :] = back[(rows - 1) * cols :]


def middle_kernel(
    halt_ref, hidden_ref, back_ref, prev_ref, next_ref, grad_ref, conv_ref,
    keep_ref, send_ref, two_ref, gtwo_ref, columns_ref,
):
    rows, _, cols = halt_ref.shape
    own = rows * cols
    width = hidden_ref.shape[1]
    core = lax.axis_index("core")

    padded = jnp.concatenate([prev_ref[0 : 2 * cols], hidden_ref[...], next_ref[0 : 2 * cols]], axis=0)
    left, right = neighbours(padded, cols)
    wide = own + 2 * cols
    for a in range(3):
        for b, shifted in enumerate((left, padded, right)):
            tap = 3 * a + b
            columns_ref[:, tap * width : (tap + 1) * width] = shifted[a * cols : a * cols + wide]
    pre_two = dot(columns_ref[...], conv_ref[...], 1, 1)
    back = jnp.concatenate([prev_ref[2 * cols :], back_ref[...], next_ref[2 * cols :]], axis=0)
    grad_two = jnp.where(pre_two > 0, back.astype(F32), 0.0).astype(BF)
    gtwo_ref[...] = grad_two
    active = active_column(halt_ref)
    hidden_two = (active * jnp.maximum(pre_two[cols : cols + own], 0.0)).astype(BF)
    two_ref[...] = hidden_two

    shape = (width, width)
    per_dp = width // (NX * NH * NL * NC)
    at = lax.broadcasted_iota(jnp.int32, shape, 0)
    j, hi, lo = at % per_dp, (at // per_dp) % NH, (at // (per_dp * NH)) % NL
    x, c = (at // (per_dp * NH * NL)) % NX, at // (per_dp * NH * NL * NX)
    wanted = dp_of(x, hi, lo, c ^ core) * per_dp + j
    shuffle = (lax.broadcasted_iota(jnp.int32, shape, 1) == wanted).astype(F32).astype(BF)
    grad_rows = dot(shuffle, grad_two[cols : cols + own], 1, 1).astype(BF)
    conv_part = dot(grad_rows, columns_ref[cols : cols + own, :], 1, 0).astype(BF)
    tall, lanes = per_dp * NH, conv_part.shape[1]
    for group in range(NX * NL):
        keep_ref[group, :, 0:lanes] = conv_part[group * tall : (group + 1) * tall]
        other = NX * NL + group
        send_ref[group, :, 0:lanes] = conv_part[other * tall : (other + 1) * tall]
    expand_part = dot(grad_ref[...], hidden_two, 0, 0).astype(BF)
    per_dp = expand_part.shape[0] // (NX * NH * NL * NC)
    for x in range(NX):
        for lo in range(NL):
            for hi in range(NH):
                first = dp_of(x, hi, lo, 0) * per_dp
                zero, one = (expand_part[first + i * per_dp : first + (i + 1) * per_dp] for i in (0, 1))
                at = slice(lanes + hi * width, lanes + (hi + 1) * width)
                keep_ref[x * NL + lo, :, at] = jnp.where(core == 0, zero, one)
                send_ref[x * NL + lo, :, at] = jnp.where(core == 0, one, zero)


def leave_kernel(
    feat_ref, grad_ref, two_ref, gtwo_ref, sign_ref, reduce_ref, conv_ref, expand_ref,
    out_ref, gin_ref, columns_ref, stacked_ref, *, cols,
):
    own = feat_ref.shape[0]
    width = two_ref.shape[1]
    out_ref[...] = (feat_ref[...].astype(F32) + dot(two_ref[...], expand_ref[...], 1, 1)).astype(BF)
    grad_two = gtwo_ref[...]
    left, right = neighbours(grad_two, cols)
    for a in range(3):
        for b, shifted in enumerate((right, grad_two, left)):
            tap = 3 * a + b
            at = slice(tap * width, (tap + 1) * width)
            columns_ref[:, at] = shifted[(2 - a) * cols : (2 - a) * cols + own]
            stacked_ref[at, :] = conv_ref[:, at]
    grad_hidden = dot(columns_ref[...], stacked_ref[...], 1, 0)
    grad_one = (grad_hidden * sign_ref[...].astype(F32)).astype(BF)
    gin_ref[...] = (grad_ref[...].astype(F32) + dot(grad_one, reduce_ref[...], 1, 0)).astype(BF)


def in_vmem(array):
    return pltpu.with_memory_space_constraint(array, pltpu.VMEM)


def call(kernel, outs, *args, scratch=(), keep=True):
    shape_of = pltpu.VMEM if keep else jax.ShapeDtypeStruct
    return pl.pallas_call(
        kernel,
        out_shape=[shape_of(shape, dtype) for shape, dtype in outs],
        scratch_shapes=list(scratch),
        compiler_params=VMEM_LIMIT,
    )(*[in_vmem(a) for a in args])


def local(features, halting_map, grad_out, weight_reduce, weight_conv, weight_expand):
    samples, rows, cols, chans = features.shape
    width = weight_reduce.shape[0]
    taps = weight_conv.shape[1]
    own = samples * rows * cols
    flat_in = features.reshape(own, chans)
    upstream = grad_out.reshape(own, chans)
    halting = halting_map.reshape(samples * rows, 1, cols)

    hidden, sign, back, up, down = call(
        enter_kernel,
        [((own, width), BF)] * 3 + [((3 * cols, width), BF)] * 2,
        halting, flat_in, upstream, weight_reduce, weight_expand,
    )
    from_prev = lax.ppermute(down, "rows", [(i, i + 1) for i in range(NZ - 1)])
    from_next = lax.ppermute(up, "rows", [(i + 1, i) for i in range(NZ - 1)])

    conv_rows, expand_rows = width // (NX * NH * NL * NC), chans // (NX * NH * NL * NC)
    lanes = taps + NH * width
    part = (NX * NL, NH * conv_rows, lanes)
    wide = own + 2 * cols
    keep, send, two, gtwo = call(
        middle_kernel,
        [(part, BF), (part, BF), ((own, width), BF), ((wide, width), BF)],
        halting, hidden, back, from_prev, from_next, upstream, weight_conv,
        scratch=[pltpu.VMEM((wide, taps), BF)],
    )

    got = lax.ppermute(send, "core", [(0, 1), (1, 0)])
    out, grad_in = call(
        functools.partial(leave_kernel, cols=cols),
        [((own, chans), BF)] * 2,
        flat_in, upstream, two, gtwo, sign, weight_reduce, weight_conv, weight_expand,
        scratch=[pltpu.VMEM((own, taps), BF), pltpu.VMEM((taps, width), BF)],
        keep=False,
    )
    total = (keep.astype(F32) + got.astype(F32)).astype(BF)
    total = lax.all_to_all(total, ("x", "y_lo"), 0, 0, tiled=True).astype(F32).sum(0)
    conv = total[:, :taps].reshape(NH, conv_rows, taps)
    expand = total[:, taps:].reshape(expand_rows // conv_rows, conv_rows, NH, width)
    expand = expand.transpose(2, 1, 0, 3).reshape(NH, conv_rows, expand_rows // conv_rows * width)
    total = jnp.concatenate([conv, expand], axis=2).astype(BF)
    total = lax.all_to_all(total, "y_hi", 0, 0, tiled=True).astype(F32).sum(0).astype(BF)
    total = jnp.broadcast_to(total[None], (NZ,) + total.shape)
    total = lax.all_to_all(total, "rows", 0, 0, tiled=True).astype(F32).sum(0)
    grad_conv = total[:, :taps]
    grad_expand = total[:, taps:].reshape(conv_rows, expand_rows // conv_rows, width)
    grad_expand = grad_expand.transpose(1, 0, 2).reshape(expand_rows, width)
    return (out.reshape(features.shape), grad_in.reshape(features.shape), grad_conv, grad_expand)


def solution(mesh):
    mesh = Mesh(mesh.devices.reshape(SIZES), AXES)
    whole = P(DP, "rows", None, None)
    in_specs = (whole, P(DP, "rows", None), whole, P(), P(), P())
    out_specs = (whole, whole, P(DP, None), P(DP, None))
    return jax.shard_map(local, mesh=mesh, in_specs=in_specs, out_specs=out_specs, check_vma=False)
```

```python
import functools

import jax
import jax.numpy as jnp
from jax import lax
from jax.experimental import pallas as pl
from jax.experimental.pallas import tpu as pltpu
from jax.sharding import Mesh, PartitionSpec as P

UNIT = 5
BF = jnp.bfloat16
F32 = jnp.float32

AXES = ("x", "y_hi", "y_lo", "core", "rows")
NX, NH, NL, NC, NZ = SIZES = (4, 4, 2, 2, 8)
DP = AXES[:4]
VMEM_LIMIT = pltpu.CompilerParams(vmem_limit_bytes=56 * 1024 * 1024)


def dp_of(x, hi, lo, core):
    return ((x * NH + hi) * NL + lo) * NC + core


def dot(left, right, left_dim, right_dim):
    return lax.dot_general(
        left, right, (((left_dim,), (right_dim,)), ((), ())), preferred_element_type=F32
    )


def active_column(halt_ref):
    rows, _, cols = halt_ref.shape
    at_row = lax.broadcasted_iota(jnp.int32, (cols, cols), 0)
    at_col = lax.broadcasted_iota(jnp.int32, (cols, cols), 1)
    parts = [
        jnp.sum(
            jnp.where((at_row == at_col) & (halt_ref[r] > UNIT), 1.0, 0.0), axis=1, keepdims=True
        )
        for r in range(rows)
    ]
    return jnp.concatenate(parts, axis=0)


def neighbours(cells, cols):
    count = cells.shape[0]
    wide = cells.astype(F32)
    col = lax.rem(lax.broadcasted_iota(jnp.int32, (count, 1), 0), cols)
    left = jnp.where(col == 0, 0.0, pltpu.roll(wide, 1, 0))
    right = jnp.where(col == cols - 1, 0.0, pltpu.roll(wide, count - 1, 0))
    return left.astype(BF), right.astype(BF)


def enter_kernel(
    halt_hbm, feat_hbm, grad_hbm, reduce_hbm, expand_hbm,
    halt_ref, feat_ref, grad_ref, reduce_ref, expand_ref,
    hidden_ref, sign_ref, back_ref, up_ref, down_ref, sems,
):
    pairs = (
        (feat_hbm, feat_ref),
        (reduce_hbm, reduce_ref),
        (halt_hbm, halt_ref),
        (grad_hbm, grad_ref),
        (expand_hbm, expand_ref),
    )
    copies = [pltpu.make_async_copy(src, dst, sems.at[i]) for i, (src, dst) in enumerate(pairs)]
    for copy in copies:
        copy.start()
    rows, _, cols = halt_ref.shape
    copies[0].wait()
    copies[1].wait()
    pre_one = dot(feat_ref[...], reduce_ref[...], 1, 1)
    hidden = jnp.maximum(pre_one, 0.0).astype(BF)
    hidden_ref[...] = hidden
    sign_ref[...] = (pre_one > 0).astype(F32).astype(BF)
    up_ref[0 : 2 * cols, :] = hidden[0 : 2 * cols]
    down_ref[0 : 2 * cols, :] = hidden[(rows - 2) * cols :]
    for copy in copies[2:]:
        copy.wait()
    back = (active_column(halt_ref) * dot(grad_ref[...], expand_ref[...], 1, 0)).astype(BF)
    back_ref[...] = back
    up_ref[2 * cols :, :] = back[0:cols]
    down_ref[2 * cols :, :] = back[(rows - 1) * cols :]


def middle_kernel(
    halt_ref, hidden_ref, back_ref, prev_ref, next_ref, grad_ref, conv_ref,
    keep_ref, send_ref, two_ref, gtwo_ref, columns_ref,
):
    rows, _, cols = halt_ref.shape
    own = rows * cols
    width = hidden_ref.shape[1]
    core = lax.axis_index("core")

    padded = jnp.concatenate([prev_ref[0 : 2 * cols], hidden_ref[...], next_ref[0 : 2 * cols]], axis=0)
    left, right = neighbours(padded, cols)
    wide = own + 2 * cols
    for a in range(3):
        for b, shifted in enumerate((left, padded, right)):
            tap = 3 * a + b
            columns_ref[:, tap * width : (tap + 1) * width] = shifted[a * cols : a * cols + wide]
    pre_two = dot(columns_ref[...], conv_ref[...], 1, 1)
    back = jnp.concatenate([prev_ref[2 * cols :], back_ref[...], next_ref[2 * cols :]], axis=0)
    grad_two = jnp.where(pre_two > 0, back.astype(F32), 0.0).astype(BF)
    gtwo_ref[...] = grad_two
    active = active_column(halt_ref)
    hidden_two = (active * jnp.maximum(pre_two[cols : cols + own], 0.0)).astype(BF)
    two_ref[...] = hidden_two

    shape = (width, width)
    per_dp = width // (NX * NH * NL * NC)
    at = lax.broadcasted_iota(jnp.int32, shape, 0)
    j, hi, lo = at % per_dp, (at // per_dp) % NH, (at // (per_dp * NH)) % NL
    x, c = (at // (per_dp * NH * NL)) % NX, at // (per_dp * NH * NL * NX)
    wanted = dp_of(x, hi, lo, c ^ core) * per_dp + j
    shuffle = (lax.broadcasted_iota(jnp.int32, shape, 1) == wanted).astype(F32).astype(BF)
    grad_rows = dot(shuffle, grad_two[cols : cols + own], 1, 1).astype(BF)
    conv_part = dot(grad_rows, columns_ref[cols : cols + own, :], 1, 0).astype(BF)
    tall, lanes = per_dp * NH, conv_part.shape[1]
    for group in range(NX * NL):
        keep_ref[group, :, 0:lanes] = conv_part[group * tall : (group + 1) * tall]
        other = NX * NL + group
        send_ref[group, :, 0:lanes] = conv_part[other * tall : (other + 1) * tall]
    expand_part = dot(grad_ref[...], hidden_two, 0, 0).astype(BF)
    per_dp = expand_part.shape[0] // (NX * NH * NL * NC)
    for x in range(NX):
        for lo in range(NL):
            for hi in range(NH):
                first = dp_of(x, hi, lo, 0) * per_dp
                zero, one = (expand_part[first + i * per_dp : first + (i + 1) * per_dp] for i in (0, 1))
                at = slice(lanes + hi * width, lanes + (hi + 1) * width)
                keep_ref[x * NL + lo, :, at] = jnp.where(core == 0, zero, one)
                send_ref[x * NL + lo, :, at] = jnp.where(core == 0, one, zero)


def leave_kernel(
    feat_ref, grad_ref, two_ref, gtwo_ref, sign_ref, reduce_ref, conv_ref, expand_ref,
    out_ref, gin_ref, done_ref, columns_ref, stacked_ref, *, cols,
):
    own = feat_ref.shape[0]
    width = two_ref.shape[1]
    out_ref[...] = (feat_ref[...].astype(F32) + dot(two_ref[...], expand_ref[...], 1, 1)).astype(BF)
    grad_two = gtwo_ref[...]
    left, right = neighbours(grad_two, cols)
    for a in range(3):
        for b, shifted in enumerate((right, grad_two, left)):
            tap = 3 * a + b
            at = slice(tap * width, (tap + 1) * width)
            columns_ref[:, at] = shifted[(2 - a) * cols : (2 - a) * cols + own]
            stacked_ref[at, :] = conv_ref[:, at]
    grad_hidden = dot(columns_ref[...], stacked_ref[...], 1, 0)
    grad_one = (grad_hidden * sign_ref[...].astype(F32)).astype(BF)
    gin_ref[...] = (grad_ref[...].astype(F32) + dot(grad_one, reduce_ref[...], 1, 0)).astype(BF)
    done_ref[...] = jnp.zeros_like(done_ref)


def sum_of(parts_ref):
    total = parts_ref[0].astype(F32)
    for i in range(1, parts_ref.shape[0]):
        total = total + parts_ref[i].astype(F32)
    return total


def core_kernel(keep_ref, got_ref, out_ref):
    out_ref[...] = (keep_ref[...].astype(F32) + got_ref[...].astype(F32)).astype(BF)


def x_kernel(got_ref, done_ref, out_ref, *, taps, width):
    total = sum_of(got_ref)
    highs, count, lanes = out_ref.shape
    for hi in range(highs):
        out_ref[hi, :, 0:taps] = total[hi * count : (hi + 1) * count, 0:taps].astype(BF)
        at = slice(taps + hi * width, taps + (hi + 1) * width)
        for q in range((lanes - taps) // width):
            to = slice(taps + q * width, taps + (q + 1) * width)
            out_ref[hi, :, to] = total[q * count : (q + 1) * count, at].astype(BF)


def y_kernel(got_ref, out_ref):
    total = sum_of(got_ref).astype(BF)
    for z in range(out_ref.shape[0]):
        out_ref[z] = total


def z_kernel(got_ref, conv_ref, expand_ref):
    total = sum_of(got_ref)
    count, taps = conv_ref.shape
    width = expand_ref.shape[1]
    conv_ref[...] = total[:, 0:taps]
    for q in range(expand_ref.shape[0] // count):
        expand_ref[q * count : (q + 1) * count, :] = total[:, taps + q * width : taps + (q + 1) * width]


def in_vmem(array):
    return pltpu.with_memory_space_constraint(array, pltpu.VMEM)


def call(kernel, outs, *args, scratch=(), **options):
    return pl.pallas_call(
        kernel,
        out_shape=outs,
        scratch_shapes=list(scratch),
        compiler_params=VMEM_LIMIT,
        **options,
    )(*[in_vmem(a) for a in args])


def local(features, halting_map, grad_out, weight_reduce, weight_conv, weight_expand):
    samples, rows, cols, chans = features.shape
    width = weight_reduce.shape[0]
    taps = weight_conv.shape[1]
    own = samples * rows * cols
    inputs = (
        halting_map.reshape(samples * rows, 1, cols),
        features.reshape(own, chans),
        grad_out.reshape(own, chans),
        weight_reduce,
        weight_expand,
    )
    halting, flat_in, upstream, reduce_in, expand_in, hidden, sign, back, up, down = pl.pallas_call(
        enter_kernel,
        out_shape=[pltpu.VMEM(a.shape, a.dtype) for a in inputs]
        + [pltpu.VMEM((own, width), BF)] * 3
        + [pltpu.VMEM((3 * cols, width), BF)] * 2,
        in_specs=[pl.BlockSpec(memory_space=pl.ANY)] * len(inputs),
        scratch_shapes=[pltpu.SemaphoreType.DMA((len(inputs),))],
        compiler_params=VMEM_LIMIT,
    )(*inputs)
    from_prev = lax.ppermute(down, "rows", [(i, i + 1) for i in range(NZ - 1)])
    from_next = lax.ppermute(up, "rows", [(i + 1, i) for i in range(NZ - 1)])

    conv_rows, expand_rows = width // (NX * NH * NL * NC), chans // (NX * NH * NL * NC)
    lanes = taps + NH * width
    part = (NX * NL, NH * conv_rows, lanes)
    wide = own + 2 * cols
    keep, send, two, gtwo = call(
        middle_kernel,
        [pltpu.VMEM(part, BF), pltpu.VMEM(part, BF), pltpu.VMEM((own, width), BF), pltpu.VMEM((wide, width), BF)],
        halting, hidden, back, from_prev, from_next, upstream, weight_conv,
        scratch=[pltpu.VMEM((wide, taps), BF)],
    )

    got = lax.ppermute(send, "core", [(0, 1), (1, 0)])
    out, grad_in, done = call(
        functools.partial(leave_kernel, cols=cols),
        [jax.ShapeDtypeStruct((own, chans), BF)] * 2 + [pltpu.VMEM((8, 128), F32)],
        flat_in, upstream, two, gtwo, sign, reduce_in, weight_conv, expand_in,
        scratch=[pltpu.VMEM((own, taps), BF), pltpu.VMEM((taps, width), BF)],
    )
    (total,) = call(core_kernel, [pltpu.VMEM(part, BF)], keep, got)
    got = lax.all_to_all(total, ("x", "y_lo"), 0, 0, tiled=True)
    shard = (conv_rows, taps + expand_rows // conv_rows * width)
    (total,) = call(
        functools.partial(x_kernel, taps=taps, width=width), [pltpu.VMEM((NH,) + shard, BF)], got, done
    )
    got = lax.all_to_all(total, "y_hi", 0, 0, tiled=True)
    (total,) = call(y_kernel, [pltpu.VMEM((NZ,) + shard, BF)], got)
    got = lax.all_to_all(total, "rows", 0, 0, tiled=True)
    grad_conv, grad_expand = call(
        z_kernel,
        [jax.ShapeDtypeStruct((conv_rows, taps), F32), jax.ShapeDtypeStruct((expand_rows, width), F32)],
        got,
    )
    return (out.reshape(features.shape), grad_in.reshape(features.shape), grad_conv, grad_expand)


def solution(mesh):
    mesh = Mesh(mesh.devices.reshape(SIZES), AXES)
    whole = P(DP, "rows", None, None)
    in_specs = (whole, P(DP, "rows", None), whole, P(), P(), P())
    out_specs = (whole, whole, P(DP, None), P(DP, None))
    return jax.shard_map(local, mesh=mesh, in_specs=in_specs, out_specs=out_specs, check_vma=False)
```

```python
import functools

import jax
import jax.numpy as jnp
from jax import lax
from jax.experimental import pallas as pl
from jax.experimental.pallas import tpu as pltpu
from jax.sharding import Mesh, PartitionSpec as P

UNIT = 5
BF = jnp.bfloat16
F32 = jnp.float32

AXES = ("x", "y_hi", "y_lo", "core", "rows")
NX, NH, NL, NC, NZ = SIZES = (4, 4, 2, 2, 8)
DP = AXES[:4]
VMEM_LIMIT = pltpu.CompilerParams(vmem_limit_bytes=20 * 1024 * 1024)


def dp_of(x, hi, lo, core):
    return ((x * NH + hi) * NL + lo) * NC + core


def dot(left, right, left_dim, right_dim):
    return lax.dot_general(
        left, right, (((left_dim,), (right_dim,)), ((), ())), preferred_element_type=F32
    )


def active_column(halt_ref):
    rows, _, cols = halt_ref.shape
    at_row = lax.broadcasted_iota(jnp.int32, (cols, cols), 0)
    at_col = lax.broadcasted_iota(jnp.int32, (cols, cols), 1)
    parts = [
        jnp.sum(
            jnp.where((at_row == at_col) & (halt_ref[r] > UNIT), 1.0, 0.0), axis=1, keepdims=True
        )
        for r in range(rows)
    ]
    return jnp.concatenate(parts, axis=0)


def neighbours(cells, cols):
    count = cells.shape[0]
    wide = cells.astype(F32)
    col = lax.rem(lax.broadcasted_iota(jnp.int32, (count, 1), 0), cols)
    left = jnp.where(col == 0, 0.0, pltpu.roll(wide, 1, 0))
    right = jnp.where(col == cols - 1, 0.0, pltpu.roll(wide, count - 1, 0))
    return left.astype(BF), right.astype(BF)


def enter_kernel(
    halt_hbm, feat_hbm, grad_hbm, reduce_hbm, expand_hbm,
    halt_ref, feat_ref, grad_ref, reduce_ref, expand_ref,
    hidden_ref, sign_ref, back_ref, up_ref, down_ref, sems,
):
    pairs = (
        (feat_hbm, feat_ref),
        (reduce_hbm, reduce_ref),
        (halt_hbm, halt_ref),
        (grad_hbm, grad_ref),
        (expand_hbm, expand_ref),
    )
    copies = [pltpu.make_async_copy(src, dst, sems.at[i]) for i, (src, dst) in enumerate(pairs)]
    for copy in copies:
        copy.start()
    rows, _, cols = halt_ref.shape
    copies[0].wait()
    copies[1].wait()
    pre_one = dot(feat_ref[...], reduce_ref[...], 1, 1)
    hidden = jnp.maximum(pre_one, 0.0).astype(BF)
    hidden_ref[...] = hidden
    sign_ref[...] = (pre_one > 0).astype(F32).astype(BF)
    up_ref[0 : 2 * cols, :] = hidden[0 : 2 * cols]
    down_ref[0 : 2 * cols, :] = hidden[(rows - 2) * cols :]
    for copy in copies[2:]:
        copy.wait()
    back = (active_column(halt_ref) * dot(grad_ref[...], expand_ref[...], 1, 0)).astype(BF)
    back_ref[...] = back
    up_ref[2 * cols :, :] = back[0:cols]
    down_ref[2 * cols :, :] = back[(rows - 1) * cols :]


def fill_columns(columns_ref, first, cells, cols):
    width = cells.shape[1]
    count = cells.shape[0] - 2 * cols
    left, right = neighbours(cells, cols)
    for a in range(3):
        for b, shifted in enumerate((left, cells, right)):
            at = slice((3 * a + b) * width, (3 * a + b + 1) * width)
            columns_ref[first : first + count, at] = shifted[a * cols : a * cols + count]


def sorting(width):
    shape = (width, width)
    per_dp = width // (NX * NH * NL * NC)
    at = lax.broadcasted_iota(jnp.int32, shape, 0)
    j, hi, lo = at % per_dp, (at // per_dp) % NH, (at // (per_dp * NH)) % NL
    x, c = (at // (per_dp * NH * NL)) % NX, at // (per_dp * NH * NL * NX)
    wanted = dp_of(x, hi, lo, c ^ lax.axis_index("core")) * per_dp + j
    return (lax.broadcasted_iota(jnp.int32, shape, 1) == wanted).astype(F32).astype(BF)


def inner_kernel(
    halt_ref, hidden_ref, back_ref, grad_ref, conv_ref,
    cpart_ref, epart_ref, two_ref, gtwo_ref, columns_ref,
):
    rows, _, cols = halt_ref.shape
    inner = slice(cols, (rows - 1) * cols)
    fill_columns(columns_ref, 0, hidden_ref[...], cols)
    pre_two = dot(columns_ref[...], conv_ref[...], 1, 1)
    grad_two = jnp.where(pre_two > 0, back_ref[inner, :].astype(F32), 0.0).astype(BF)
    gtwo_ref[...] = grad_two
    hidden_two = (active_column(halt_ref)[inner] * jnp.maximum(pre_two, 0.0)).astype(BF)
    two_ref[...] = hidden_two
    grad_rows = dot(sorting(grad_two.shape[1]), grad_two, 1, 1).astype(BF)
    cpart_ref[...] = dot(grad_rows, columns_ref[...], 1, 0)
    epart_ref[...] = dot(grad_ref[inner, :], hidden_two, 0, 0)


def outer_kernel(
    halt_ref, hidden_ref, back_ref, prev_ref, next_ref, grad_ref, conv_ref, cpart_ref, epart_ref,
    keep_ref, send_ref, two_ref, gtwo_ref, columns_ref,
):
    rows, _, cols = halt_ref.shape
    width = hidden_ref.shape[1]
    core = lax.axis_index("core")
    top, end = slice(0, cols), slice((rows - 1) * cols, rows * cols)
    halo = 2 * cols
    above = jnp.concatenate([prev_ref[0:halo], hidden_ref[0:halo]], axis=0)
    below = jnp.concatenate([hidden_ref[(rows - 2) * cols :], next_ref[0:halo]], axis=0)
    fill_columns(columns_ref, 0, above, cols)
    fill_columns(columns_ref, halo, below, cols)
    pre_two = dot(columns_ref[...], conv_ref[...], 1, 1)
    back = jnp.concatenate([prev_ref[halo:], back_ref[top, :], back_ref[end, :], next_ref[halo:]], axis=0)
    grad_two = jnp.where(pre_two > 0, back.astype(F32), 0.0).astype(BF)
    gtwo_ref[...] = grad_two
    active = active_column(halt_ref)
    active = jnp.concatenate([active[top], active[end]], axis=0)
    own = slice(cols, cols + halo)
    hidden_two = (active * jnp.maximum(pre_two[own], 0.0)).astype(BF)
    two_ref[...] = hidden_two

    grad_rows = dot(sorting(width), grad_two[own], 1, 1).astype(BF)
    conv_part = (cpart_ref[...] + dot(grad_rows, columns_ref[own, :], 1, 0)).astype(BF)
    per_dp, lanes = width // (NX * NH * NL * NC), conv_part.shape[1]
    tall = per_dp * NH
    for group in range(NX * NL):
        keep_ref[group, :, 0:lanes] = conv_part[group * tall : (group + 1) * tall]
        other = NX * NL + group
        send_ref[group, :, 0:lanes] = conv_part[other * tall : (other + 1) * tall]
    upstream = jnp.concatenate([grad_ref[top, :], grad_ref[end, :]], axis=0)
    expand_part = (epart_ref[...] + dot(upstream, hidden_two, 0, 0)).astype(BF)
    per_dp = expand_part.shape[0] // (NX * NH * NL * NC)
    for x in range(NX):
        for lo in range(NL):
            for hi in range(NH):
                first = dp_of(x, hi, lo, 0) * per_dp
                zero, one = (expand_part[first + i * per_dp : first + (i + 1) * per_dp] for i in (0, 1))
                at = slice(lanes + hi * width, lanes + (hi + 1) * width)
                keep_ref[x * NL + lo, :, at] = jnp.where(core == 0, zero, one)
                send_ref[x * NL + lo, :, at] = jnp.where(core == 0, one, zero)


def leave_kernel(
    feat_ref, grad_ref, two_in_ref, two_ref, gtwo_in_ref, gtwo_ref, sign_ref, reduce_ref, conv_ref, expand_ref,
    out_ref, gin_ref, done_ref, columns_ref, stacked_ref, *, cols,
):
    own = feat_ref.shape[0]
    width = two_ref.shape[1]
    two = jnp.concatenate([two_ref[0:cols], two_in_ref[...], two_ref[cols:]], axis=0)
    out_ref[...] = (feat_ref[...].astype(F32) + dot(two, expand_ref[...], 1, 1)).astype(BF)
    grad_two = jnp.concatenate([gtwo_ref[0 : 2 * cols], gtwo_in_ref[...], gtwo_ref[2 * cols :]], axis=0)
    left, right = neighbours(grad_two, cols)
    for a in range(3):
        for b, shifted in enumerate((right, grad_two, left)):
            tap = 3 * a + b
            at = slice(tap * width, (tap + 1) * width)
            columns_ref[:, at] = shifted[(2 - a) * cols : (2 - a) * cols + own]
            stacked_ref[at, :] = conv_ref[:, at]
    grad_hidden = dot(columns_ref[...], stacked_ref[...], 1, 0)
    grad_one = (grad_hidden * sign_ref[...].astype(F32)).astype(BF)
    gin_ref[...] = (grad_ref[...].astype(F32) + dot(grad_one, reduce_ref[...], 1, 0)).astype(BF)
    done_ref[...] = jnp.zeros_like(done_ref)


def sum_of(parts_ref):
    total = parts_ref[0].astype(F32)
    for i in range(1, parts_ref.shape[0]):
        total = total + parts_ref[i].astype(F32)
    return total


def core_kernel(keep_ref, got_ref, out_ref):
    out_ref[...] = (keep_ref[...].astype(F32) + got_ref[...].astype(F32)).astype(BF)


def x_kernel(got_ref, done_ref, out_ref, *, taps, width):
    total = sum_of(got_ref)
    highs, count, lanes = out_ref.shape
    for hi in range(highs):
        out_ref[hi, :, 0:taps] = total[hi * count : (hi + 1) * count, 0:taps].astype(BF)
        at = slice(taps + hi * width, taps + (hi + 1) * width)
        for q in range((lanes - taps) // width):
            to = slice(taps + q * width, taps + (q + 1) * width)
            out_ref[hi, :, to] = total[q * count : (q + 1) * count, at].astype(BF)


def y_kernel(got_ref, out_ref):
    total = sum_of(got_ref).astype(BF)
    for z in range(out_ref.shape[0]):
        out_ref[z] = total


def z_kernel(got_ref, conv_ref, expand_ref):
    total = sum_of(got_ref)
    count, taps = conv_ref.shape
    width = expand_ref.shape[1]
    conv_ref[...] = total[:, 0:taps]
    for q in range(expand_ref.shape[0] // count):
        expand_ref[q * count : (q + 1) * count, :] = total[:, taps + q * width : taps + (q + 1) * width]


def in_vmem(array):
    return pltpu.with_memory_space_constraint(array, pltpu.VMEM)


def call(kernel, outs, *args, scratch=(), **options):
    return pl.pallas_call(
        kernel,
        out_shape=outs,
        scratch_shapes=list(scratch),
        compiler_params=VMEM_LIMIT,
        **options,
    )(*[in_vmem(a) for a in args])


def local(features, halting_map, grad_out, weight_reduce, weight_conv, weight_expand):
    samples, rows, cols, chans = features.shape
    width = weight_reduce.shape[0]
    taps = weight_conv.shape[1]
    own = samples * rows * cols
    inputs = (
        halting_map.reshape(samples * rows, 1, cols),
        features.reshape(own, chans),
        grad_out.reshape(own, chans),
        weight_reduce,
        weight_expand,
    )
    halting, flat_in, upstream, reduce_in, expand_in, hidden, sign, back, up, down = pl.pallas_call(
        enter_kernel,
        out_shape=[pltpu.VMEM(a.shape, a.dtype) for a in inputs]
        + [pltpu.VMEM((own, width), BF)] * 3
        + [pltpu.VMEM((3 * cols, width), BF)] * 2,
        in_specs=[pl.BlockSpec(memory_space=pl.ANY)] * len(inputs),
        scratch_shapes=[pltpu.SemaphoreType.DMA((len(inputs),))],
        compiler_params=VMEM_LIMIT,
    )(*[pltpu.with_memory_space_constraint(a, pltpu.MemorySpace.HBM) for a in inputs])
    from_prev = lax.ppermute(down, "rows", [(i, i + 1) for i in range(NZ - 1)])
    from_next = lax.ppermute(up, "rows", [(i + 1, i) for i in range(NZ - 1)])

    conv_rows, expand_rows = width // (NX * NH * NL * NC), chans // (NX * NH * NL * NC)
    lanes = taps + NH * width
    part = (NX * NL, NH * conv_rows, lanes)
    inner = (own - 2 * cols, width)
    conv_part, expand_part, two_in, gtwo_in = call(
        inner_kernel,
        [pltpu.VMEM((width, taps), F32), pltpu.VMEM((chans, width), F32), pltpu.VMEM(inner, BF), pltpu.VMEM(inner, BF)],
        halting, hidden, back, upstream, weight_conv,
        scratch=[pltpu.VMEM((inner[0], taps), BF)],
    )
    keep, send, two, gtwo = call(
        outer_kernel,
        [pltpu.VMEM(part, BF), pltpu.VMEM(part, BF), pltpu.VMEM((2 * cols, width), BF), pltpu.VMEM((4 * cols, width), BF)],
        halting, hidden, back, from_prev, from_next, upstream, weight_conv, conv_part, expand_part,
        scratch=[pltpu.VMEM((4 * cols, taps), BF)],
    )

    got = lax.ppermute(send, "core", [(0, 1), (1, 0)])
    out, grad_in, done = call(
        functools.partial(leave_kernel, cols=cols),
        [jax.ShapeDtypeStruct((own, chans), BF)] * 2 + [pltpu.VMEM((8, 128), F32)],
        flat_in, upstream, two_in, two, gtwo_in, gtwo, sign, reduce_in, weight_conv, expand_in,
        scratch=[pltpu.VMEM((own, taps), BF), pltpu.VMEM((taps, width), BF)],
    )
    (total,) = call(core_kernel, [pltpu.VMEM(part, BF)], keep, got)
    got = lax.all_to_all(total, ("x", "y_lo"), 0, 0, tiled=True)
    shard = (conv_rows, taps + expand_rows // conv_rows * width)
    (total,) = call(
        functools.partial(x_kernel, taps=taps, width=width), [pltpu.VMEM((NH,) + shard, BF)], got, done
    )
    got = lax.all_to_all(total, "y_hi", 0, 0, tiled=True)
    (total,) = call(y_kernel, [pltpu.VMEM((NZ,) + shard, BF)], got)
    got = lax.all_to_all(total, "rows", 0, 0, tiled=True)
    grad_conv, grad_expand = call(
        z_kernel,
        [jax.ShapeDtypeStruct((conv_rows, taps), F32), jax.ShapeDtypeStruct((expand_rows, width), F32)],
        got,
    )
    return (out.reshape(features.shape), grad_in.reshape(features.shape), grad_conv, grad_expand)


def solution(mesh):
    mesh = Mesh(mesh.devices.reshape(SIZES), AXES)
    whole = P(DP, "rows", None, None)
    in_specs = (whole, P(DP, "rows", None), whole, P(), P(), P())
    out_specs = (whole, whole, P(DP, None), P(DP, None))
    return jax.shard_map(local, mesh=mesh, in_specs=in_specs, out_specs=out_specs, check_vma=False)
```

```python
import functools

import jax
import jax.numpy as jnp
from jax import lax
from jax.experimental import pallas as pl
from jax.experimental.pallas import tpu as pltpu
from jax.sharding import Mesh, PartitionSpec as P

UNIT = 5
BF = jnp.bfloat16
F32 = jnp.float32

AXES = ("x", "y_hi", "y_lo", "core", "rows")
NX, NH, NL, NC, NZ = SIZES = (4, 4, 2, 2, 8)
DP = AXES[:4]
VMEM_LIMIT = pltpu.CompilerParams(vmem_limit_bytes=20 * 1024 * 1024)


def dp_of(x, hi, lo, core):
    return ((x * NH + hi) * NL + lo) * NC + core


def dot(left, right, left_dim, right_dim):
    return lax.dot_general(
        left, right, (((left_dim,), (right_dim,)), ((), ())), preferred_element_type=F32
    )


def active_column(halt_ref, rows):
    cols = halt_ref.shape[2]
    at_row = lax.broadcasted_iota(jnp.int32, (cols, cols), 0)
    at_col = lax.broadcasted_iota(jnp.int32, (cols, cols), 1)
    parts = [
        jnp.sum(
            jnp.where((at_row == at_col) & (halt_ref[r] > UNIT), 1.0, 0.0), axis=1, keepdims=True
        )
        for r in rows
    ]
    return jnp.concatenate(parts, axis=0)


def neighbours(cells, cols):
    count = cells.shape[0]
    wide = cells.astype(F32)
    col = lax.broadcasted_iota(jnp.int32, (count, 1), 0) & (cols - 1)
    left = jnp.where(col == 0, 0.0, pltpu.roll(wide, 1, 0))
    right = jnp.where(col == cols - 1, 0.0, pltpu.roll(wide, count - 1, 0))
    return left.astype(BF), right.astype(BF)


def enter_kernel(
    halt_hbm, feat_hbm, grad_hbm, reduce_hbm, expand_hbm,
    halt_ref, feat_ref, grad_ref, reduce_ref, expand_ref,
    hidden_ref, sign_ref, back_ref, up_ref, down_ref, sems,
):
    pairs = (
        (feat_hbm, feat_ref),
        (reduce_hbm, reduce_ref),
        (halt_hbm, halt_ref),
        (grad_hbm, grad_ref),
        (expand_hbm, expand_ref),
    )
    copies = [pltpu.make_async_copy(src, dst, sems.at[i]) for i, (src, dst) in enumerate(pairs)]
    for copy in copies:
        copy.start()
    rows, _, cols = halt_ref.shape
    copies[0].wait()
    copies[1].wait()
    pre_one = dot(feat_ref[...], reduce_ref[...], 1, 1)
    hidden = jnp.maximum(pre_one, 0.0).astype(BF)
    hidden_ref[...] = hidden
    sign_ref[...] = (pre_one > 0).astype(F32).astype(BF)
    up_ref[0 : 2 * cols, :] = hidden[0 : 2 * cols]
    down_ref[0 : 2 * cols, :] = hidden[(rows - 2) * cols :]
    for copy in copies[2:]:
        copy.wait()
    back = (active_column(halt_ref, range(rows)) * dot(grad_ref[...], expand_ref[...], 1, 0)).astype(BF)
    back_ref[...] = back
    up_ref[2 * cols :, :] = back[0:cols]
    down_ref[2 * cols :, :] = back[(rows - 1) * cols :]


def fill_columns(columns_ref, first, cells, cols):
    width = cells.shape[1]
    count = cells.shape[0] - 2 * cols
    left, right = neighbours(cells, cols)
    for a in range(3):
        for b, shifted in enumerate((left, cells, right)):
            at = slice((3 * a + b) * width, (3 * a + b + 1) * width)
            columns_ref[first : first + count, at] = shifted[a * cols : a * cols + count]


def sorting(width):
    at = lax.broadcasted_iota(jnp.int32, (width, 1), 0)
    j, hi, lo = at & 3, (at >> 2) & (NH - 1), (at >> 4) & (NL - 1)
    x, c = (at >> 5) & (NX - 1), at >> 7
    wanted = dp_of(x, hi, lo, c ^ lax.axis_index("core")) * 4 + j
    channel = lax.broadcasted_iota(jnp.int32, (width, width), 1)
    return (channel == wanted).astype(F32).astype(BF)


def inner_kernel(
    halt_ref, hidden_ref, back_ref, grad_ref, conv_ref,
    cpart_ref, epart_ref, two_ref, gtwo_ref, columns_ref,
):
    rows, _, cols = halt_ref.shape
    inner = slice(cols, (rows - 1) * cols)
    fill_columns(columns_ref, 0, hidden_ref[...], cols)
    pre_two = dot(columns_ref[...], conv_ref[...], 1, 1)
    grad_two = jnp.where(pre_two > 0, back_ref[inner, :].astype(F32), 0.0).astype(BF)
    gtwo_ref[...] = grad_two
    hidden_two = (active_column(halt_ref, range(1, rows - 1)) * jnp.maximum(pre_two, 0.0)).astype(BF)
    two_ref[...] = hidden_two
    grad_rows = dot(sorting(grad_two.shape[1]), grad_two, 1, 1).astype(BF)
    cpart_ref[...] = dot(grad_rows, columns_ref[...], 1, 0)
    epart_ref[...] = dot(grad_ref[inner, :], hidden_two, 0, 0)


def outer_kernel(
    halt_ref, hidden_ref, back_ref, prev_ref, next_ref, grad_ref, conv_ref, cpart_ref, epart_ref,
    keep_ref, send_ref, two_ref, gtwo_ref, columns_ref,
):
    rows, _, cols = halt_ref.shape
    width = hidden_ref.shape[1]
    core = lax.axis_index("core")
    top, end = slice(0, cols), slice((rows - 1) * cols, rows * cols)
    halo = 2 * cols
    above = jnp.concatenate([prev_ref[0:halo], hidden_ref[0:halo]], axis=0)
    below = jnp.concatenate([hidden_ref[(rows - 2) * cols :], next_ref[0:halo]], axis=0)
    fill_columns(columns_ref, 0, above, cols)
    fill_columns(columns_ref, halo, below, cols)
    pre_two = dot(columns_ref[...], conv_ref[...], 1, 1)
    back = jnp.concatenate([prev_ref[halo:], back_ref[top, :], back_ref[end, :], next_ref[halo:]], axis=0)
    grad_two = jnp.where(pre_two > 0, back.astype(F32), 0.0).astype(BF)
    gtwo_ref[...] = grad_two
    active = active_column(halt_ref, (0, rows - 1))
    own = slice(cols, cols + halo)
    hidden_two = (active * jnp.maximum(pre_two[own], 0.0)).astype(BF)
    two_ref[...] = hidden_two

    grad_rows = dot(sorting(width), grad_two[own], 1, 1).astype(BF)
    conv_part = (cpart_ref[...] + dot(grad_rows, columns_ref[own, :], 1, 0)).astype(BF)
    tall = width // (NX * NL * NC)
    taps = conv_part.shape[1] // width
    for group in range(NX * NL):
        other = NX * NL + group
        for tap in range(taps):
            to, at = slice(tap * tall, (tap + 1) * tall), slice(tap * width, (tap + 1) * width)
            keep_ref[group, to, :] = conv_part[group * tall : (group + 1) * tall, at]
            send_ref[group, to, :] = conv_part[other * tall : (other + 1) * tall, at]
    upstream = jnp.concatenate([grad_ref[top, :], grad_ref[end, :]], axis=0)
    expand_part = (epart_ref[...] + dot(upstream, hidden_two, 0, 0)).astype(BF)
    per_dp = expand_part.shape[0] // (NX * NH * NL * NC)
    for x in range(NX):
        for lo in range(NL):
            for hi in range(NH):
                first = dp_of(x, hi, lo, 0) * per_dp
                zero, one = (expand_part[first + i * per_dp : first + (i + 1) * per_dp] for i in (0, 1))
                to = slice(taps * tall + hi * per_dp, taps * tall + (hi + 1) * per_dp)
                keep_ref[x * NL + lo, to, :] = jnp.where(core == 0, zero, one)
                send_ref[x * NL + lo, to, :] = jnp.where(core == 0, one, zero)


def leave_kernel(
    feat_ref, grad_ref, two_in_ref, two_ref, gtwo_in_ref, gtwo_ref, sign_ref, reduce_ref, conv_ref, expand_ref,
    out_ref, gin_ref, done_ref, columns_ref, stacked_ref, *, cols,
):
    own = feat_ref.shape[0]
    width = two_ref.shape[1]
    two = jnp.concatenate([two_ref[0:cols], two_in_ref[...], two_ref[cols:]], axis=0)
    out_ref[...] = (feat_ref[...].astype(F32) + dot(two, expand_ref[...], 1, 1)).astype(BF)
    grad_two = jnp.concatenate([gtwo_ref[0 : 2 * cols], gtwo_in_ref[...], gtwo_ref[2 * cols :]], axis=0)
    left, right = neighbours(grad_two, cols)
    for a in range(3):
        for b, shifted in enumerate((right, grad_two, left)):
            tap = 3 * a + b
            at = slice(tap * width, (tap + 1) * width)
            columns_ref[:, at] = shifted[(2 - a) * cols : (2 - a) * cols + own]
            stacked_ref[at, :] = conv_ref[:, at]
    grad_hidden = dot(columns_ref[...], stacked_ref[...], 1, 0)
    grad_one = (grad_hidden * sign_ref[...].astype(F32)).astype(BF)
    gin_ref[...] = (grad_ref[...].astype(F32) + dot(grad_one, reduce_ref[...], 1, 0)).astype(BF)
    done_ref[...] = jnp.zeros_like(done_ref)


def sum_of(parts_ref):
    total = parts_ref[0].astype(F32)
    for i in range(1, parts_ref.shape[0]):
        total = total + parts_ref[i].astype(F32)
    return total


def core_kernel(keep_ref, got_ref, done_ref, out_ref):
    out_ref[...] = (keep_ref[...].astype(F32) + got_ref[...].astype(F32)).astype(BF)


def x_kernel(got_ref, out_ref, *, taps):
    total = sum_of(got_ref).astype(BF)
    highs, count, lanes = out_ref.shape
    width = total.shape[1]
    blocks = lanes // width
    for hi in range(highs):
        for i in range(blocks):
            if i < taps:
                first = (i * highs + hi) * count
            else:
                first = (taps * highs + hi * (blocks - taps) + i - taps) * count
            out_ref[hi, :, i * width : (i + 1) * width] = total[first : first + count]


def y_kernel(got_ref, out_ref):
    total = sum_of(got_ref).astype(BF)
    for z in range(out_ref.shape[0]):
        out_ref[z] = total


def z_kernel(got_ref, conv_ref, expand_ref):
    total = sum_of(got_ref)
    count, taps = conv_ref.shape
    width = expand_ref.shape[1]
    conv_ref[...] = total[:, 0:taps]
    for q in range(expand_ref.shape[0] // count):
        expand_ref[q * count : (q + 1) * count, :] = total[:, taps + q * width : taps + (q + 1) * width]


def in_vmem(array):
    return pltpu.with_memory_space_constraint(array, pltpu.VMEM)


def call(kernel, outs, *args, scratch=(), **options):
    return pl.pallas_call(
        kernel,
        out_shape=outs,
        scratch_shapes=list(scratch),
        compiler_params=VMEM_LIMIT,
        **options,
    )(*[in_vmem(a) for a in args])


def local(features, halting_map, grad_out, weight_reduce, weight_conv, weight_expand):
    samples, rows, cols, chans = features.shape
    width = weight_reduce.shape[0]
    taps = weight_conv.shape[1]
    own = samples * rows * cols
    inputs = (
        halting_map.reshape(samples * rows, 1, cols),
        features.reshape(own, chans),
        grad_out.reshape(own, chans),
        weight_reduce,
        weight_expand,
    )
    halting, flat_in, upstream, reduce_in, expand_in, hidden, sign, back, up, down = pl.pallas_call(
        enter_kernel,
        out_shape=[pltpu.VMEM(a.shape, a.dtype) for a in inputs]
        + [pltpu.VMEM((own, width), BF)] * 3
        + [pltpu.VMEM((3 * cols, width), BF)] * 2,
        in_specs=[pl.BlockSpec(memory_space=pl.ANY)] * len(inputs),
        scratch_shapes=[pltpu.SemaphoreType.DMA((len(inputs),))],
        compiler_params=VMEM_LIMIT,
    )(*[pltpu.with_memory_space_constraint(a, pltpu.MemorySpace.HBM) for a in inputs])
    from_prev = lax.ppermute(down, "rows", [(i, i + 1) for i in range(NZ - 1)])
    from_next = lax.ppermute(up, "rows", [(i + 1, i) for i in range(NZ - 1)])

    conv_rows, expand_rows = width // (NX * NH * NL * NC), chans // (NX * NH * NL * NC)
    part = (NX * NL, NH * (conv_rows * taps // width + expand_rows), width)
    inner = (own - 2 * cols, width)
    conv_part, expand_part, two_in, gtwo_in = call(
        inner_kernel,
        [pltpu.VMEM((width, taps), F32), pltpu.VMEM((chans, width), F32), pltpu.VMEM(inner, BF), pltpu.VMEM(inner, BF)],
        halting, hidden, back, upstream, weight_conv,
        scratch=[pltpu.VMEM((inner[0], taps), BF)],
    )
    keep, send, two, gtwo = call(
        outer_kernel,
        [pltpu.VMEM(part, BF), pltpu.VMEM(part, BF), pltpu.VMEM((2 * cols, width), BF), pltpu.VMEM((4 * cols, width), BF)],
        halting, hidden, back, from_prev, from_next, upstream, weight_conv, conv_part, expand_part,
        scratch=[pltpu.VMEM((4 * cols, taps), BF)],
    )

    got = lax.ppermute(send, "core", [(0, 1), (1, 0)])
    out, grad_in, done = call(
        functools.partial(leave_kernel, cols=cols),
        [jax.ShapeDtypeStruct((own, chans), BF)] * 2 + [pltpu.VMEM((8, 128), F32)],
        flat_in, upstream, two_in, two, gtwo_in, gtwo, sign, reduce_in, weight_conv, expand_in,
        scratch=[pltpu.VMEM((own, taps), BF), pltpu.VMEM((taps, width), BF)],
    )
    (total,) = call(core_kernel, [pltpu.VMEM(part, BF)], keep, got, done)
    got = lax.all_to_all(total, ("x", "y_lo"), 0, 0, tiled=True)
    shard = (conv_rows, taps + expand_rows // conv_rows * width)
    (total,) = call(
        functools.partial(x_kernel, taps=taps // width), [pltpu.VMEM((NH,) + shard, BF)], got
    )
    got = lax.all_to_all(total, "y_hi", 0, 0, tiled=True)
    (total,) = call(y_kernel, [pltpu.VMEM((NZ,) + shard, BF)], got)
    got = lax.all_to_all(total, "rows", 0, 0, tiled=True)
    grad_conv, grad_expand = call(
        z_kernel,
        [jax.ShapeDtypeStruct((conv_rows, taps), F32), jax.ShapeDtypeStruct((expand_rows, width), F32)],
        got,
    )
    return (out.reshape(features.shape), grad_in.reshape(features.shape), grad_conv, grad_expand)


def solution(mesh):
    mesh = Mesh(mesh.devices.reshape(SIZES), AXES)
    whole = P(DP, "rows", None, None)
    in_specs = (whole, P(DP, "rows", None), whole, P(), P(), P())
    out_specs = (whole, whole, P(DP, None), P(DP, None))
    return jax.shard_map(local, mesh=mesh, in_specs=in_specs, out_specs=out_specs, check_vma=False)
```

```python
import functools

import jax
import jax.numpy as jnp
from jax import lax
from jax.experimental import pallas as pl
from jax.experimental.pallas import tpu as pltpu
from jax.sharding import Mesh, PartitionSpec as P

UNIT = 5
BF = jnp.bfloat16
F32 = jnp.float32

AXES = ("x_hi", "x_lo", "y_hi", "y_lo", "core", "rows")
SIZES = (2, 2, 4, 2, 2, 8)
DP = AXES[:5]
NX, NY, NC, NZ = 4, 8, 2, 8
HX, HY, HZ = NX // 2, NY // 2, NZ // 2
VMEM_LIMIT = pltpu.CompilerParams(vmem_limit_bytes=20 * 1024 * 1024)


def dp_of(x, y, core):
    return (x * NY + y) * NC + core


def squares():
    def member(block, parity, size, core):
        return (2 * block + parity) % size if core == 0 or parity == 1 else (2 * block + 2) % size

    return [
        [dp_of(member(bx, i, NX, core), member(by, j, NY, core), core) for i in (0, 1) for j in (0, 1)]
        for core in range(NC)
        for bx in range(HX)
        for by in range(HY)
    ]


def rest():
    return [
        [
            dp_of(2 * x_hi + x, 2 * y_hi + y, core) * NZ + 2 * z + low
            for x_hi in range(HX)
            for y_hi in range(HY)
            for low in range(2)
        ]
        for x in range(2)
        for y in range(2)
        for core in range(NC)
        for z in range(HZ)
    ]


def dot(left, right, left_dim, right_dim):
    return lax.dot_general(
        left, right, (((left_dim,), (right_dim,)), ((), ())), preferred_element_type=F32
    )


def active_column(halt_ref, rows):
    cols = halt_ref.shape[2]
    at_row = lax.broadcasted_iota(jnp.int32, (cols, cols), 0)
    at_col = lax.broadcasted_iota(jnp.int32, (cols, cols), 1)
    parts = [
        jnp.sum(
            jnp.where((at_row == at_col) & (halt_ref[r] > UNIT), 1.0, 0.0), axis=1, keepdims=True
        )
        for r in rows
    ]
    return jnp.concatenate(parts, axis=0)


def neighbours(cells, cols):
    count = cells.shape[0]
    wide = cells.astype(F32)
    col = lax.broadcasted_iota(jnp.int32, (count, 1), 0) & (cols - 1)
    left = jnp.where(col == 0, 0.0, pltpu.roll(wide, 1, 0))
    right = jnp.where(col == cols - 1, 0.0, pltpu.roll(wide, count - 1, 0))
    return left.astype(BF), right.astype(BF)


def enter_kernel(
    halt_hbm, feat_hbm, grad_hbm, reduce_hbm, expand_hbm,
    halt_ref, feat_ref, grad_ref, reduce_ref, expand_ref,
    hidden_ref, sign_ref, back_ref, up_ref, down_ref, sems,
):
    pairs = (
        (feat_hbm, feat_ref),
        (reduce_hbm, reduce_ref),
        (halt_hbm, halt_ref),
        (grad_hbm, grad_ref),
        (expand_hbm, expand_ref),
    )
    copies = [pltpu.make_async_copy(src, dst, sems.at[i]) for i, (src, dst) in enumerate(pairs)]
    for copy in copies:
        copy.start()
    rows, _, cols = halt_ref.shape
    copies[0].wait()
    copies[1].wait()
    pre_one = dot(feat_ref[...], reduce_ref[...], 1, 1)
    hidden = jnp.maximum(pre_one, 0.0).astype(BF)
    hidden_ref[...] = hidden
    sign_ref[...] = (pre_one > 0).astype(F32).astype(BF)
    up_ref[0 : 2 * cols, :] = hidden[0 : 2 * cols]
    down_ref[0 : 2 * cols, :] = hidden[(rows - 2) * cols :]
    for copy in copies[2:]:
        copy.wait()
    back = (active_column(halt_ref, range(rows)) * dot(grad_ref[...], expand_ref[...], 1, 0)).astype(BF)
    back_ref[...] = back
    up_ref[2 * cols :, :] = back[0:cols]
    down_ref[2 * cols :, :] = back[(rows - 1) * cols :]


def fill_columns(columns_ref, first, cells, cols):
    width = cells.shape[1]
    count = cells.shape[0] - 2 * cols
    left, right = neighbours(cells, cols)
    for a in range(3):
        for b, shifted in enumerate((left, cells, right)):
            at = slice((3 * a + b) * width, (3 * a + b + 1) * width)
            columns_ref[first : first + count, at] = shifted[a * cols : a * cols + count]


def sorting(width):
    at = lax.broadcasted_iota(jnp.int32, (width, 1), 0)
    j, y_hi, x_hi = at & 3, (at >> 2) & (HY - 1), (at >> 4) & (HX - 1)
    y_lo, x_lo, c = (at >> 5) & 1, (at >> 6) & 1, at >> 7
    wanted = dp_of(2 * x_hi + x_lo, 2 * y_hi + y_lo, c ^ lax.axis_index("core")) * 4 + j
    channel = lax.broadcasted_iota(jnp.int32, (width, width), 1)
    return (channel == wanted).astype(F32).astype(BF)


def inner_kernel(
    halt_ref, hidden_ref, back_ref, grad_ref, conv_ref,
    cpart_ref, epart_ref, two_ref, gtwo_ref, columns_ref,
):
    rows, _, cols = halt_ref.shape
    inner = slice(cols, (rows - 1) * cols)
    fill_columns(columns_ref, 0, hidden_ref[...], cols)
    pre_two = dot(columns_ref[...], conv_ref[...], 1, 1)
    grad_two = jnp.where(pre_two > 0, back_ref[inner, :].astype(F32), 0.0).astype(BF)
    gtwo_ref[...] = grad_two
    hidden_two = (active_column(halt_ref, range(1, rows - 1)) * jnp.maximum(pre_two, 0.0)).astype(BF)
    two_ref[...] = hidden_two
    grad_rows = dot(sorting(grad_two.shape[1]), grad_two, 1, 1).astype(BF)
    cpart_ref[...] = dot(grad_rows, columns_ref[...], 1, 0)
    epart_ref[...] = dot(grad_ref[inner, :], hidden_two, 0, 0)


def outer_kernel(
    halt_ref, hidden_ref, back_ref, prev_ref, next_ref, grad_ref, conv_ref, cpart_ref, epart_ref,
    keep_ref, send_ref, two_ref, gtwo_ref, columns_ref,
):
    rows, _, cols = halt_ref.shape
    width = hidden_ref.shape[1]
    core = lax.axis_index("core")
    top, end = slice(0, cols), slice((rows - 1) * cols, rows * cols)
    halo = 2 * cols
    above = jnp.concatenate([prev_ref[0:halo], hidden_ref[0:halo]], axis=0)
    below = jnp.concatenate([hidden_ref[(rows - 2) * cols :], next_ref[0:halo]], axis=0)
    fill_columns(columns_ref, 0, above, cols)
    fill_columns(columns_ref, halo, below, cols)
    pre_two = dot(columns_ref[...], conv_ref[...], 1, 1)
    back = jnp.concatenate([prev_ref[halo:], back_ref[top, :], back_ref[end, :], next_ref[halo:]], axis=0)
    grad_two = jnp.where(pre_two > 0, back.astype(F32), 0.0).astype(BF)
    gtwo_ref[...] = grad_two
    active = active_column(halt_ref, (0, rows - 1))
    own = slice(cols, cols + halo)
    hidden_two = (active * jnp.maximum(pre_two[own], 0.0)).astype(BF)
    two_ref[...] = hidden_two

    grad_rows = dot(sorting(width), grad_two[own], 1, 1).astype(BF)
    conv_part = (cpart_ref[...] + dot(grad_rows, columns_ref[own, :], 1, 0)).astype(BF)
    tall = width // 8
    taps = conv_part.shape[1] // width
    for place in range(4):
        other = 4 + place
        for tap in range(taps):
            to, at = slice(tap * tall, (tap + 1) * tall), slice(tap * width, (tap + 1) * width)
            keep_ref[place, to, :] = conv_part[place * tall : (place + 1) * tall, at]
            send_ref[place, to, :] = conv_part[other * tall : (other + 1) * tall, at]
    upstream = jnp.concatenate([grad_ref[top, :], grad_ref[end, :]], axis=0)
    expand_part = (epart_ref[...] + dot(upstream, hidden_two, 0, 0)).astype(BF)
    per_dp = expand_part.shape[0] // (NX * NY * NC)
    for x in range(NX):
        for y in range(NY):
            first = dp_of(x, y, 0) * per_dp
            zero, one = (expand_part[first + i * per_dp : first + (i + 1) * per_dp] for i in (0, 1))
            mine, theirs = jnp.where(core == 0, zero, one), jnp.where(core == 0, one, zero)
            start = taps * tall + (x // 2 * HY + y // 2) * per_dp
            place = x % 2 * 2 + y % 2
            keep_ref[place, start : start + per_dp, :] = mine
            send_ref[place, start : start + per_dp, :] = theirs


def leave_kernel(
    feat_ref, grad_ref, two_in_ref, two_ref, gtwo_in_ref, gtwo_ref, sign_ref, reduce_ref, conv_ref, expand_ref,
    out_ref, gin_ref, done_ref, columns_ref, stacked_ref, *, cols,
):
    own = feat_ref.shape[0]
    width = two_ref.shape[1]
    two = jnp.concatenate([two_ref[0:cols], two_in_ref[...], two_ref[cols:]], axis=0)
    out_ref[...] = (feat_ref[...].astype(F32) + dot(two, expand_ref[...], 1, 1)).astype(BF)
    grad_two = jnp.concatenate([gtwo_ref[0 : 2 * cols], gtwo_in_ref[...], gtwo_ref[2 * cols :]], axis=0)
    left, right = neighbours(grad_two, cols)
    for a in range(3):
        for b, shifted in enumerate((right, grad_two, left)):
            tap = 3 * a + b
            at = slice(tap * width, (tap + 1) * width)
            columns_ref[:, at] = shifted[(2 - a) * cols : (2 - a) * cols + own]
            stacked_ref[at, :] = conv_ref[:, at]
    grad_hidden = dot(columns_ref[...], stacked_ref[...], 1, 0)
    grad_one = (grad_hidden * sign_ref[...].astype(F32)).astype(BF)
    gin_ref[...] = (grad_ref[...].astype(F32) + dot(grad_one, reduce_ref[...], 1, 0)).astype(BF)
    done_ref[...] = jnp.zeros_like(done_ref)


def sum_of(parts_ref):
    total = parts_ref[0].astype(F32)
    for i in range(1, parts_ref.shape[0]):
        total = total + parts_ref[i].astype(F32)
    return total


def core_kernel(keep_ref, got_ref, done_ref, out_ref):
    out_ref[...] = (keep_ref[...].astype(F32) + got_ref[...].astype(F32)).astype(BF)


def square_kernel(got_ref, out_ref, *, taps):
    total = sum_of(got_ref).astype(BF)
    parts, count, lanes = out_ref.shape
    half = total.shape[1] // 2
    shards, blocks = parts // 2, lanes // half
    for shard in range(shards):
        for i in range(blocks):
            if i < taps:
                first = (i * shards + shard) * count
            else:
                first = (taps * shards + shard * (blocks - taps) + i - taps) * count
            for low in range(2):
                block = total[first : first + count, low * half : (low + 1) * half]
                out_ref[2 * shard + low, :, i * half : (i + 1) * half] = block


def plane_kernel(got_ref, out_ref):
    total = sum_of(got_ref).astype(BF)
    for z in range(out_ref.shape[0]):
        out_ref[z] = total


def rows_kernel(got_ref, conv_ref, expand_ref):
    count, width = conv_ref.shape[0], expand_ref.shape[1]
    half, taps = width // 2, conv_ref.shape[1] // width
    for low in range(2):
        total = got_ref[low].astype(F32)
        for z in range(low + 2, NZ, 2):
            total = total + got_ref[z].astype(F32)
        for i in range(got_ref.shape[2] // half):
            block = total[:, i * half : (i + 1) * half]
            if i < taps:
                conv_ref[:, i * width + low * half : i * width + (low + 1) * half] = block
            else:
                first = (i - taps) * count
                expand_ref[first : first + count, low * half : (low + 1) * half] = block


def in_vmem(array):
    return pltpu.with_memory_space_constraint(array, pltpu.VMEM)


def call(kernel, outs, *args, scratch=(), **options):
    return pl.pallas_call(
        kernel,
        out_shape=outs,
        scratch_shapes=list(scratch),
        compiler_params=VMEM_LIMIT,
        **options,
    )(*[in_vmem(a) for a in args])


def local(features, halting_map, grad_out, weight_reduce, weight_conv, weight_expand):
    samples, rows, cols, chans = features.shape
    width = weight_reduce.shape[0]
    taps = weight_conv.shape[1]
    own = samples * rows * cols
    inputs = (
        halting_map.reshape(samples * rows, 1, cols),
        features.reshape(own, chans),
        grad_out.reshape(own, chans),
        weight_reduce,
        weight_expand,
    )
    halting, flat_in, upstream, reduce_in, expand_in, hidden, sign, back, up, down = pl.pallas_call(
        enter_kernel,
        out_shape=[pltpu.VMEM(a.shape, a.dtype) for a in inputs]
        + [pltpu.VMEM((own, width), BF)] * 3
        + [pltpu.VMEM((3 * cols, width), BF)] * 2,
        in_specs=[pl.BlockSpec(memory_space=pl.ANY)] * len(inputs),
        scratch_shapes=[pltpu.SemaphoreType.DMA((len(inputs),))],
        compiler_params=VMEM_LIMIT,
    )(*[pltpu.with_memory_space_constraint(a, pltpu.MemorySpace.HBM) for a in inputs])
    from_prev = lax.ppermute(down, "rows", [(i, i + 1) for i in range(NZ - 1)])
    from_next = lax.ppermute(up, "rows", [(i + 1, i) for i in range(NZ - 1)])

    devices = NX * NY * NC
    conv_rows, expand_rows = width // devices, chans // devices
    shard_rows = conv_rows * taps // width + expand_rows
    part = (4, HX * HY * shard_rows, width)
    inner = (own - 2 * cols, width)
    conv_part, expand_part, two_in, gtwo_in = call(
        inner_kernel,
        [pltpu.VMEM((width, taps), F32), pltpu.VMEM((chans, width), F32), pltpu.VMEM(inner, BF), pltpu.VMEM(inner, BF)],
        halting, hidden, back, upstream, weight_conv,
        scratch=[pltpu.VMEM((inner[0], taps), BF)],
    )
    keep, send, two, gtwo = call(
        outer_kernel,
        [pltpu.VMEM(part, BF), pltpu.VMEM(part, BF), pltpu.VMEM((2 * cols, width), BF), pltpu.VMEM((4 * cols, width), BF)],
        halting, hidden, back, from_prev, from_next, upstream, weight_conv, conv_part, expand_part,
        scratch=[pltpu.VMEM((4 * cols, taps), BF)],
    )

    got = lax.ppermute(send, "core", [(0, 1), (1, 0)])
    out, grad_in, done = call(
        functools.partial(leave_kernel, cols=cols),
        [jax.ShapeDtypeStruct((own, chans), BF)] * 2 + [pltpu.VMEM((8, 128), F32)],
        flat_in, upstream, two_in, two, gtwo_in, gtwo, sign, reduce_in, weight_conv, expand_in,
        scratch=[pltpu.VMEM((own, taps), BF), pltpu.VMEM((taps, width), BF)],
    )
    (total,) = call(core_kernel, [pltpu.VMEM(part, BF)], keep, got, done)
    got = lax.all_to_all(total, DP, 0, 0, axis_index_groups=squares(), tiled=True)
    shard = (conv_rows, shard_rows // conv_rows * width // 2)
    (total,) = call(
        functools.partial(square_kernel, taps=taps // width), [pltpu.VMEM((2 * HX * HY,) + shard, BF)], got
    )
    got = lax.all_to_all(total, AXES, 0, 0, axis_index_groups=rest(), tiled=True)
    (total,) = call(plane_kernel, [pltpu.VMEM((NZ,) + shard, BF)], got)
    got = lax.all_to_all(total, "rows", 0, 0, tiled=True)
    grad_conv, grad_expand = call(
        rows_kernel,
        [jax.ShapeDtypeStruct((conv_rows, taps), F32), jax.ShapeDtypeStruct((expand_rows, width), F32)],
        got,
    )
    return (out.reshape(features.shape), grad_in.reshape(features.shape), grad_conv, grad_expand)


def solution(mesh):
    mesh = Mesh(mesh.devices.reshape(SIZES), AXES)
    whole = P(DP, "rows", None, None)
    in_specs = (whole, P(DP, "rows", None), whole, P(), P(), P())
    out_specs = (whole, whole, P(DP, None), P(DP, None))
    return jax.shard_map(local, mesh=mesh, in_specs=in_specs, out_specs=out_specs, check_vma=False)
```

```python
import functools

import jax
import jax.numpy as jnp
from jax import lax
from jax.experimental import pallas as pl
from jax.experimental.pallas import tpu as pltpu
from jax.sharding import Mesh, PartitionSpec as P

UNIT = 5
BF = jnp.bfloat16
F32 = jnp.float32

AXES = ("x_hi", "x_lo", "y_hi", "y_lo", "core", "rows")
SIZES = (2, 2, 4, 2, 2, 8)
DP = AXES[:5]
NX, NY, NC, NZ = 4, 8, 2, 8
HX, HY, HZ = NX // 2, NY // 2, NZ // 2
VMEM_LIMIT = pltpu.CompilerParams(vmem_limit_bytes=20 * 1024 * 1024)


def dp_of(x, y, core):
    return (x * NY + y) * NC + core


def near_groups():
    along_x = [
        [dp_of(x, y, 0) * NZ + z for x in range(NX)]
        for y in range(NY)
        for z in range(NZ)
    ]
    squares = [
        [dp_of(x, 2 * y_hi + i, 1) * NZ + 2 * z_hi + k for i in (0, 1) for k in (0, 1)]
        for x in range(NX)
        for y_hi in range(HY)
        for z_hi in range(HZ)
    ]
    return along_x + squares


def far_groups():
    columns = [
        [dp_of(x, y, 0) * NZ + 2 * z_hi + k for y in range(NY) for k in (0, 1)]
        for x in range(NX)
        for z_hi in range(HZ)
    ]
    planes = [
        [dp_of(x, 2 * y_hi + i, 1) * NZ + z for x in range(NX) for y_hi in range(HY)]
        for i in (0, 1)
        for z in range(NZ)
    ]
    return columns + planes


def dot(left, right, left_dim, right_dim):
    return lax.dot_general(
        left, right, (((left_dim,), (right_dim,)), ((), ())), preferred_element_type=F32
    )


def active_column(halt_ref, rows):
    cols = halt_ref.shape[2]
    at_row = lax.broadcasted_iota(jnp.int32, (cols, cols), 0)
    at_col = lax.broadcasted_iota(jnp.int32, (cols, cols), 1)
    parts = [
        jnp.sum(
            jnp.where((at_row == at_col) & (halt_ref[r] > UNIT), 1.0, 0.0), axis=1, keepdims=True
        )
        for r in rows
    ]
    return jnp.concatenate(parts, axis=0)


def neighbours(cells, cols):
    count = cells.shape[0]
    wide = cells.astype(F32)
    col = lax.broadcasted_iota(jnp.int32, (count, 1), 0) & (cols - 1)
    left = jnp.where(col == 0, 0.0, pltpu.roll(wide, 1, 0))
    right = jnp.where(col == cols - 1, 0.0, pltpu.roll(wide, count - 1, 0))
    return left.astype(BF), right.astype(BF)


def enter_kernel(
    halt_hbm, feat_hbm, grad_hbm, reduce_hbm, expand_hbm,
    halt_ref, feat_ref, grad_ref, reduce_ref, expand_ref,
    hidden_ref, sign_ref, back_ref, up_ref, down_ref, sems,
):
    pairs = (
        (feat_hbm, feat_ref),
        (reduce_hbm, reduce_ref),
        (halt_hbm, halt_ref),
        (grad_hbm, grad_ref),
        (expand_hbm, expand_ref),
    )
    copies = [pltpu.make_async_copy(src, dst, sems.at[i]) for i, (src, dst) in enumerate(pairs)]
    for copy in copies:
        copy.start()
    rows, _, cols = halt_ref.shape
    copies[0].wait()
    copies[1].wait()
    pre_one = dot(feat_ref[...], reduce_ref[...], 1, 1)
    hidden = jnp.maximum(pre_one, 0.0).astype(BF)
    hidden_ref[...] = hidden
    sign_ref[...] = (pre_one > 0).astype(F32).astype(BF)
    up_ref[0 : 2 * cols, :] = hidden[0 : 2 * cols]
    down_ref[0 : 2 * cols, :] = hidden[(rows - 2) * cols :]
    for copy in copies[2:]:
        copy.wait()
    edges = jnp.concatenate([grad_ref[0:cols, :], grad_ref[(rows - 1) * cols :, :]], axis=0)
    back = (active_column(halt_ref, (0, rows - 1)) * dot(edges, expand_ref[...], 1, 0)).astype(BF)
    back_ref[...] = back
    up_ref[2 * cols :, :] = back[0:cols]
    down_ref[2 * cols :, :] = back[cols:]


def fill_columns(columns_ref, first, cells, cols):
    width = cells.shape[1]
    count = cells.shape[0] - 2 * cols
    left, right = neighbours(cells, cols)
    for a in range(3):
        for b, shifted in enumerate((left, cells, right)):
            at = slice((3 * a + b) * width, (3 * a + b + 1) * width)
            columns_ref[first : first + count, at] = shifted[a * cols : a * cols + count]


def sorting(width):
    at = lax.broadcasted_iota(jnp.int32, (width, 1), 0)
    j, place, c = at & 3, (at >> 2) & (NX * NY - 1), at >> 7
    x, y = place >> 3, place & (NY - 1)
    other_x, other_y = (place >> 2) & (NX - 1), 2 * (place & (HY - 1)) + (place >> 4)
    wanted = jnp.where(c == 0, dp_of(x, y, 0), dp_of(other_x, other_y, 1)) * 4 + j
    channel = lax.broadcasted_iota(jnp.int32, (width, width), 1)
    return (channel == wanted).astype(F32).astype(BF)


def inner_kernel(
    halt_ref, hidden_ref, grad_ref, expand_ref, conv_ref,
    cpart_ref, epart_ref, two_ref, gtwo_ref, columns_ref,
):
    rows, _, cols = halt_ref.shape
    inner = slice(cols, (rows - 1) * cols)
    fill_columns(columns_ref, 0, hidden_ref[...], cols)
    pre_two = dot(columns_ref[...], conv_ref[...], 1, 1)
    back = active_column(halt_ref, range(1, rows - 1)) * dot(grad_ref[inner, :], expand_ref[...], 1, 0)
    grad_two = jnp.where(pre_two > 0, back, 0.0).astype(BF)
    gtwo_ref[...] = grad_two
    hidden_two = (active_column(halt_ref, range(1, rows - 1)) * jnp.maximum(pre_two, 0.0)).astype(BF)
    two_ref[...] = hidden_two
    grad_rows = dot(sorting(grad_two.shape[1]), grad_two, 1, 1).astype(BF)
    cpart_ref[...] = dot(grad_rows, columns_ref[...], 1, 0)
    epart_ref[...] = dot(grad_ref[inner, :], hidden_two, 0, 0)


def outer_kernel(
    halt_ref, hidden_ref, back_ref, prev_ref, next_ref, grad_ref, conv_ref, cpart_ref, epart_ref,
    keep_ref, send_ref, two_ref, gtwo_ref, columns_ref,
):
    rows, _, cols = halt_ref.shape
    width = hidden_ref.shape[1]
    core = lax.axis_index("core")
    top, end = slice(0, cols), slice((rows - 1) * cols, rows * cols)
    halo = 2 * cols
    above = jnp.concatenate([prev_ref[0:halo], hidden_ref[0:halo]], axis=0)
    below = jnp.concatenate([hidden_ref[(rows - 2) * cols :], next_ref[0:halo]], axis=0)
    fill_columns(columns_ref, 0, above, cols)
    fill_columns(columns_ref, halo, below, cols)
    pre_two = dot(columns_ref[...], conv_ref[...], 1, 1)
    back = jnp.concatenate([prev_ref[halo:], back_ref[...], next_ref[halo:]], axis=0)
    grad_two = jnp.where(pre_two > 0, back.astype(F32), 0.0).astype(BF)
    gtwo_ref[...] = grad_two
    active = active_column(halt_ref, (0, rows - 1))
    own = slice(cols, cols + halo)
    hidden_two = (active * jnp.maximum(pre_two[own], 0.0)).astype(BF)
    two_ref[...] = hidden_two

    grad_rows = dot(sorting(width), grad_two[own], 1, 1).astype(BF)
    conv_part = (cpart_ref[...] + dot(grad_rows, columns_ref[own, :], 1, 0)).astype(BF)
    upstream = jnp.concatenate([grad_ref[top, :], grad_ref[end, :]], axis=0)
    expand_part = (epart_ref[...] + dot(upstream, hidden_two, 0, 0)).astype(BF)

    def write(group, rows, low, zero, one):
        at = slice(low * half, (low + 1) * half)
        keep_ref[group, rows, at] = jnp.where(core == 0, zero, one)
        send_ref[group, rows, at] = jnp.where(core == 0, one, zero)

    tall, taps, half = width // 8, conv_part.shape[1] // width, width // 2
    per_dp = expand_part.shape[0] // (NX * NY * NC)
    for group in range(4):
        y_lo, part = group // 2, group % 2
        for low in range(2):
            zero = conv_part[group * tall : (group + 1) * tall]
            first = (4 + 2 * y_lo + low) * tall
            one = conv_part[first : first + tall]
            for tap in range(taps):
                lanes = tap * width + low * half, tap * width + part * half
                rows = slice(tap * tall, (tap + 1) * tall)
                write(group, rows, low, zero[:, lanes[0] : lanes[0] + half], one[:, lanes[1] : lanes[1] + half])
            for shard in range(NY):
                first = dp_of(group, shard, 0) * per_dp
                zero_part = expand_part[first : first + per_dp, low * half : (low + 1) * half]
                first = dp_of(2 * low + shard // HY, 2 * (shard % HY) + y_lo, 1) * per_dp
                one_part = expand_part[first : first + per_dp, part * half : (part + 1) * half]
                start = taps * tall + shard * per_dp
                write(group, slice(start, start + per_dp), low, zero_part, one_part)


def leave_kernel(
    feat_ref, grad_ref, two_in_ref, two_ref, gtwo_in_ref, gtwo_ref, sign_ref, reduce_ref, conv_ref, expand_ref,
    out_ref, gin_ref, done_ref, columns_ref, stacked_ref, *, cols,
):
    own = feat_ref.shape[0]
    width = two_ref.shape[1]
    two = jnp.concatenate([two_ref[0:cols], two_in_ref[...], two_ref[cols:]], axis=0)
    out_ref[...] = (feat_ref[...].astype(F32) + dot(two, expand_ref[...], 1, 1)).astype(BF)
    grad_two = jnp.concatenate([gtwo_ref[0 : 2 * cols], gtwo_in_ref[...], gtwo_ref[2 * cols :]], axis=0)
    left, right = neighbours(grad_two, cols)
    for a in range(3):
        for b, shifted in enumerate((right, grad_two, left)):
            tap = 3 * a + b
            at = slice(tap * width, (tap + 1) * width)
            columns_ref[:, at] = shifted[(2 - a) * cols : (2 - a) * cols + own]
            stacked_ref[at, :] = conv_ref[:, at]
    grad_hidden = dot(columns_ref[...], stacked_ref[...], 1, 0)
    grad_one = (grad_hidden * sign_ref[...].astype(F32)).astype(BF)
    gin_ref[...] = (grad_ref[...].astype(F32) + dot(grad_one, reduce_ref[...], 1, 0)).astype(BF)
    done_ref[...] = jnp.zeros_like(done_ref)


def sum_of(parts_ref):
    total = parts_ref[0].astype(F32)
    for i in range(1, parts_ref.shape[0]):
        total = total + parts_ref[i].astype(F32)
    return total


def core_kernel(keep_ref, got_ref, done_ref, out_ref):
    out_ref[...] = (keep_ref[...].astype(F32) + got_ref[...].astype(F32)).astype(BF)


def near_kernel(got_ref, out_ref, *, taps):
    total = sum_of(got_ref).astype(BF)
    core = lax.axis_index("core")
    parts, count, lanes = out_ref.shape
    half = total.shape[1] // 2
    shards, blocks = parts // 2, lanes // half
    for shard in range(shards):
        for low in range(2):
            to = jnp.where(core == 0, 2 * shard + low, shards * low + shard)
            for i in range(blocks):
                if i < taps:
                    first = (i * shards + shard) * count
                else:
                    first = (taps * shards + shard * (blocks - taps) + i - taps) * count
                block = total[first : first + count, low * half : (low + 1) * half]
                out_ref[to, :, i * half : (i + 1) * half] = block


def plane_kernel(got_ref, out_ref):
    total = sum_of(got_ref).astype(BF)
    for z in range(out_ref.shape[0]):
        out_ref[z] = total


def rows_kernel(got_ref, conv_ref, expand_ref):
    count, width = conv_ref.shape[0], expand_ref.shape[1]
    half, taps = width // 2, conv_ref.shape[1] // width
    for low in range(2):
        total = got_ref[low].astype(F32)
        for z in range(low + 2, NZ, 2):
            total = total + got_ref[z].astype(F32)
        for i in range(got_ref.shape[2] // half):
            block = total[:, i * half : (i + 1) * half]
            if i < taps:
                conv_ref[:, i * width + low * half : i * width + (low + 1) * half] = block
            else:
                first = (i - taps) * count
                expand_ref[first : first + count, low * half : (low + 1) * half] = block


def in_vmem(array):
    return pltpu.with_memory_space_constraint(array, pltpu.VMEM)


def call(kernel, outs, *args, scratch=(), **options):
    return pl.pallas_call(
        kernel,
        out_shape=outs,
        scratch_shapes=list(scratch),
        compiler_params=VMEM_LIMIT,
        **options,
    )(*[in_vmem(a) for a in args])


def local(features, halting_map, grad_out, weight_reduce, weight_conv, weight_expand):
    samples, rows, cols, chans = features.shape
    width = weight_reduce.shape[0]
    taps = weight_conv.shape[1]
    own = samples * rows * cols
    inputs = (
        halting_map.reshape(samples * rows, 1, cols),
        features.reshape(own, chans),
        grad_out.reshape(own, chans),
        weight_reduce,
        weight_expand,
    )
    halting, flat_in, upstream, reduce_in, expand_in, hidden, sign, back, up, down = pl.pallas_call(
        enter_kernel,
        out_shape=[pltpu.VMEM(a.shape, a.dtype) for a in inputs]
        + [pltpu.VMEM((own, width), BF)] * 2
        + [pltpu.VMEM((2 * cols, width), BF)]
        + [pltpu.VMEM((3 * cols, width), BF)] * 2,
        in_specs=[pl.BlockSpec(memory_space=pl.ANY)] * len(inputs),
        scratch_shapes=[pltpu.SemaphoreType.DMA((len(inputs),))],
        compiler_params=VMEM_LIMIT,
    )(*[pltpu.with_memory_space_constraint(a, pltpu.MemorySpace.HBM) for a in inputs])
    from_prev = lax.ppermute(down, "rows", [(i, i + 1) for i in range(NZ - 1)])
    from_next = lax.ppermute(up, "rows", [(i + 1, i) for i in range(NZ - 1)])

    devices = NX * NY * NC
    conv_rows, expand_rows = width // devices, chans // devices
    shard_rows = conv_rows * taps // width + expand_rows
    part = (4, HX * HY * shard_rows, width)
    inner = (own - 2 * cols, width)
    conv_part, expand_part, two_in, gtwo_in = call(
        inner_kernel,
        [pltpu.VMEM((width, taps), F32), pltpu.VMEM((chans, width), F32), pltpu.VMEM(inner, BF), pltpu.VMEM(inner, BF)],
        halting, hidden, upstream, expand_in, weight_conv,
        scratch=[pltpu.VMEM((inner[0], taps), BF)],
    )
    keep, send, two, gtwo = call(
        outer_kernel,
        [pltpu.VMEM(part, BF), pltpu.VMEM(part, BF), pltpu.VMEM((2 * cols, width), BF), pltpu.VMEM((4 * cols, width), BF)],
        halting, hidden, back, from_prev, from_next, upstream, weight_conv, conv_part, expand_part,
        scratch=[pltpu.VMEM((4 * cols, taps), BF)],
    )

    got = lax.ppermute(send, "core", [(0, 1), (1, 0)])
    out, grad_in, done = call(
        functools.partial(leave_kernel, cols=cols),
        [jax.ShapeDtypeStruct((own, chans), BF)] * 2 + [pltpu.VMEM((8, 128), F32)],
        flat_in, upstream, two_in, two, gtwo_in, gtwo, sign, reduce_in, weight_conv, expand_in,
        scratch=[pltpu.VMEM((own, taps), BF), pltpu.VMEM((taps, width), BF)],
    )
    (total,) = call(core_kernel, [pltpu.VMEM(part, BF)], keep, got, done)
    got = lax.all_to_all(total, AXES, 0, 0, axis_index_groups=near_groups(), tiled=True)
    shard = (conv_rows, shard_rows // conv_rows * width // 2)
    (total,) = call(
        functools.partial(near_kernel, taps=taps // width), [pltpu.VMEM((2 * HX * HY,) + shard, BF)], got
    )
    got = lax.all_to_all(total, AXES, 0, 0, axis_index_groups=far_groups(), tiled=True)
    (total,) = call(plane_kernel, [pltpu.VMEM((NZ,) + shard, BF)], got)
    got = lax.all_to_all(total, "rows", 0, 0, tiled=True)
    grad_conv, grad_expand = call(
        rows_kernel,
        [jax.ShapeDtypeStruct((conv_rows, taps), F32), jax.ShapeDtypeStruct((expand_rows, width), F32)],
        got,
    )
    return (out.reshape(features.shape), grad_in.reshape(features.shape), grad_conv, grad_expand)


def solution(mesh):
    mesh = Mesh(mesh.devices.reshape(SIZES), AXES)
    whole = P(DP, "rows", None, None)
    in_specs = (whole, P(DP, "rows", None), whole, P(), P(), P())
    out_specs = (whole, whole, P(DP, None), P(DP, None))
    return jax.shard_map(local, mesh=mesh, in_specs=in_specs, out_specs=out_specs, check_vma=False)
```

```python
import functools

import jax
import jax.numpy as jnp
from jax import lax
from jax.experimental import pallas as pl
from jax.experimental.pallas import tpu as pltpu
from jax.sharding import Mesh, PartitionSpec as P

UNIT = 5
BF = jnp.bfloat16
F32 = jnp.float32

AXES = ("x_hi", "x_lo", "y_hi", "y_lo", "core", "rows")
SIZES = (2, 2, 4, 2, 2, 8)
DP = AXES[:5]
NX, NY, NC, NZ = 4, 8, 2, 8
HX, HY, HZ = NX // 2, NY // 2, NZ // 2
VMEM_LIMIT = pltpu.CompilerParams(vmem_limit_bytes=20 * 1024 * 1024)


def dp_of(x, y, core):
    return (x * NY + y) * NC + core


def near_groups():
    along_x = [
        [dp_of(x, y, 1) * NZ + z for x in range(NX)]
        for y in range(NY)
        for z in range(NZ)
    ]
    squares = [
        [dp_of(x, 2 * y_hi + i, 0) * NZ + 2 * z_hi + k for i in (0, 1) for k in (0, 1)]
        for x in range(NX)
        for y_hi in range(HY)
        for z_hi in range(HZ)
    ]
    return along_x + squares


def far_groups():
    columns = [
        [dp_of(x, y, 1) * NZ + 2 * z_hi + k for y in range(NY) for k in (0, 1)]
        for x in range(NX)
        for z_hi in range(HZ)
    ]
    planes = [
        [dp_of(x, 2 * y_hi + i, 0) * NZ + z for x in range(NX) for y_hi in range(HY)]
        for i in (0, 1)
        for z in range(NZ)
    ]
    return columns + planes


def dot(left, right, left_dim, right_dim):
    return lax.dot_general(
        left, right, (((left_dim,), (right_dim,)), ((), ())), preferred_element_type=F32
    )


def active_column(halt_ref, rows):
    cols = halt_ref.shape[2]
    at_row = lax.broadcasted_iota(jnp.int32, (cols, cols), 0)
    at_col = lax.broadcasted_iota(jnp.int32, (cols, cols), 1)
    parts = [
        jnp.sum(
            jnp.where((at_row == at_col) & (halt_ref[r] > UNIT), 1.0, 0.0), axis=1, keepdims=True
        )
        for r in rows
    ]
    return jnp.concatenate(parts, axis=0)


def neighbours(cells, cols):
    count = cells.shape[0]
    wide = cells.astype(F32)
    col = lax.broadcasted_iota(jnp.int32, (count, 1), 0) & (cols - 1)
    left = jnp.where(col == 0, 0.0, pltpu.roll(wide, 1, 0))
    right = jnp.where(col == cols - 1, 0.0, pltpu.roll(wide, count - 1, 0))
    return left.astype(BF), right.astype(BF)


def enter_kernel(
    halt_hbm, feat_hbm, grad_hbm, reduce_hbm, expand_hbm,
    halt_ref, feat_ref, grad_ref, reduce_ref, expand_ref,
    hidden_ref, sign_ref, back_ref, up_ref, down_ref, sems,
):
    pairs = (
        (feat_hbm, feat_ref),
        (reduce_hbm, reduce_ref),
        (halt_hbm, halt_ref),
        (grad_hbm, grad_ref),
        (expand_hbm, expand_ref),
    )
    copies = [pltpu.make_async_copy(src, dst, sems.at[i]) for i, (src, dst) in enumerate(pairs)]
    for copy in copies:
        copy.start()
    rows, _, cols = halt_ref.shape
    copies[0].wait()
    copies[1].wait()
    pre_one = dot(feat_ref[...], reduce_ref[...], 1, 1)
    hidden = jnp.maximum(pre_one, 0.0).astype(BF)
    hidden_ref[...] = hidden
    sign_ref[...] = (pre_one > 0).astype(F32).astype(BF)
    up_ref[0 : 2 * cols, :] = hidden[0 : 2 * cols]
    down_ref[0 : 2 * cols, :] = hidden[(rows - 2) * cols :]
    for copy in copies[2:]:
        copy.wait()
    edges = jnp.concatenate([grad_ref[0:cols, :], grad_ref[(rows - 1) * cols :, :]], axis=0)
    back = (active_column(halt_ref, (0, rows - 1)) * dot(edges, expand_ref[...], 1, 0)).astype(BF)
    back_ref[...] = back
    up_ref[2 * cols :, :] = back[0:cols]
    down_ref[2 * cols :, :] = back[cols:]


def fill_columns(columns_ref, first, cells, cols):
    width = cells.shape[1]
    count = cells.shape[0] - 2 * cols
    left, right = neighbours(cells, cols)
    for a in range(3):
        for b, shifted in enumerate((left, cells, right)):
            at = slice((3 * a + b) * width, (3 * a + b + 1) * width)
            columns_ref[first : first + count, at] = shifted[a * cols : a * cols + count]


def sorting(width):
    at = lax.broadcasted_iota(jnp.int32, (width, 1), 0)
    j, place, c = at & 3, (at >> 2) & (NX * NY - 1), at >> 7
    x, y = place >> 3, place & (NY - 1)
    other_x, other_y = (place >> 2) & (NX - 1), 2 * (place & (HY - 1)) + (place >> 4)
    wanted = jnp.where(c == 1, dp_of(x, y, 1), dp_of(other_x, other_y, 0)) * 4 + j
    channel = lax.broadcasted_iota(jnp.int32, (width, width), 1)
    return (channel == wanted).astype(F32).astype(BF)


def inner_kernel(
    halt_ref, hidden_ref, grad_ref, expand_ref, conv_ref,
    cpart_ref, epart_ref, two_ref, gtwo_ref, columns_ref,
):
    rows, _, cols = halt_ref.shape
    inner = slice(cols, (rows - 1) * cols)
    fill_columns(columns_ref, 0, hidden_ref[...], cols)
    pre_two = dot(columns_ref[...], conv_ref[...], 1, 1)
    back = active_column(halt_ref, range(1, rows - 1)) * dot(grad_ref[inner, :], expand_ref[...], 1, 0)
    grad_two = jnp.where(pre_two > 0, back, 0.0).astype(BF)
    gtwo_ref[...] = grad_two
    hidden_two = (active_column(halt_ref, range(1, rows - 1)) * jnp.maximum(pre_two, 0.0)).astype(BF)
    two_ref[...] = hidden_two
    grad_rows = dot(sorting(grad_two.shape[1]), grad_two, 1, 1).astype(BF)
    cpart_ref[...] = dot(grad_rows, columns_ref[...], 1, 0)
    epart_ref[...] = dot(grad_ref[inner, :], hidden_two, 0, 0)


def outer_kernel(
    halt_ref, hidden_ref, back_ref, prev_ref, next_ref, grad_ref, conv_ref, cpart_ref, epart_ref,
    keep_ref, send_ref, two_ref, gtwo_ref, columns_ref,
):
    rows, _, cols = halt_ref.shape
    width = hidden_ref.shape[1]
    core = lax.axis_index("core")
    top, end = slice(0, cols), slice((rows - 1) * cols, rows * cols)
    halo = 2 * cols
    above = jnp.concatenate([prev_ref[0:halo], hidden_ref[0:halo]], axis=0)
    below = jnp.concatenate([hidden_ref[(rows - 2) * cols :], next_ref[0:halo]], axis=0)
    fill_columns(columns_ref, 0, above, cols)
    fill_columns(columns_ref, halo, below, cols)
    pre_two = dot(columns_ref[...], conv_ref[...], 1, 1)
    back = jnp.concatenate([prev_ref[halo:], back_ref[...], next_ref[halo:]], axis=0)
    grad_two = jnp.where(pre_two > 0, back.astype(F32), 0.0).astype(BF)
    gtwo_ref[...] = grad_two
    active = active_column(halt_ref, (0, rows - 1))
    own = slice(cols, cols + halo)
    hidden_two = (active * jnp.maximum(pre_two[own], 0.0)).astype(BF)
    two_ref[...] = hidden_two

    grad_rows = dot(sorting(width), grad_two[own], 1, 1).astype(BF)
    conv_part = (cpart_ref[...] + dot(grad_rows, columns_ref[own, :], 1, 0)).astype(BF)
    upstream = jnp.concatenate([grad_ref[top, :], grad_ref[end, :]], axis=0)
    expand_part = (epart_ref[...] + dot(upstream, hidden_two, 0, 0)).astype(BF)

    def write(group, rows, low, along, square):
        at = slice(low * half, (low + 1) * half)
        keep_ref[group, rows, at] = jnp.where(core == 1, along, square)
        send_ref[group, rows, at] = jnp.where(core == 1, square, along)

    tall, taps, half = width // 8, conv_part.shape[1] // width, width // 2
    per_dp = expand_part.shape[0] // (NX * NY * NC)
    for group in range(4):
        y_lo, part = group // 2, group % 2
        for low in range(2):
            along = conv_part[(4 + group) * tall : (5 + group) * tall]
            first = (2 * y_lo + low) * tall
            square = conv_part[first : first + tall]
            for tap in range(taps):
                lanes = tap * width + low * half, tap * width + part * half
                rows = slice(tap * tall, (tap + 1) * tall)
                write(group, rows, low, along[:, lanes[0] : lanes[0] + half], square[:, lanes[1] : lanes[1] + half])
            for shard in range(NY):
                first = dp_of(group, shard, 1) * per_dp
                along_part = expand_part[first : first + per_dp, low * half : (low + 1) * half]
                first = dp_of(2 * low + shard // HY, 2 * (shard % HY) + y_lo, 0) * per_dp
                square_part = expand_part[first : first + per_dp, part * half : (part + 1) * half]
                start = taps * tall + shard * per_dp
                write(group, slice(start, start + per_dp), low, along_part, square_part)


def leave_kernel(
    feat_ref, grad_ref, two_in_ref, two_ref, gtwo_in_ref, gtwo_ref, sign_ref, reduce_ref, conv_ref, expand_ref,
    out_ref, gin_ref, done_ref, columns_ref, stacked_ref, *, cols,
):
    own = feat_ref.shape[0]
    width = two_ref.shape[1]
    two = jnp.concatenate([two_ref[0:cols], two_in_ref[...], two_ref[cols:]], axis=0)
    out_ref[...] = (feat_ref[...].astype(F32) + dot(two, expand_ref[...], 1, 1)).astype(BF)
    grad_two = jnp.concatenate([gtwo_ref[0 : 2 * cols], gtwo_in_ref[...], gtwo_ref[2 * cols :]], axis=0)
    left, right = neighbours(grad_two, cols)
    for a in range(3):
        for b, shifted in enumerate((right, grad_two, left)):
            tap = 3 * a + b
            at = slice(tap * width, (tap + 1) * width)
            columns_ref[:, at] = shifted[(2 - a) * cols : (2 - a) * cols + own]
            stacked_ref[at, :] = conv_ref[:, at]
    grad_hidden = dot(columns_ref[...], stacked_ref[...], 1, 0)
    grad_one = (grad_hidden * sign_ref[...].astype(F32)).astype(BF)
    gin_ref[...] = (grad_ref[...].astype(F32) + dot(grad_one, reduce_ref[...], 1, 0)).astype(BF)
    done_ref[...] = jnp.zeros_like(done_ref)


def sum_of(parts_ref):
    total = parts_ref[0].astype(F32)
    for i in range(1, parts_ref.shape[0]):
        total = total + parts_ref[i].astype(F32)
    return total


def core_kernel(keep_ref, got_ref, done_ref, out_ref):
    out_ref[...] = (keep_ref[...].astype(F32) + got_ref[...].astype(F32)).astype(BF)


def near_kernel(got_ref, out_ref, *, taps):
    total = sum_of(got_ref)
    core = lax.axis_index("core")
    parts, count, lanes = out_ref.shape
    half = total.shape[1] // 2
    shards, blocks = parts // 2, lanes // half
    for shard in range(shards):
        for low in range(2):
            to = jnp.where(core == 1, 2 * shard + low, shards * low + shard)
            for i in range(blocks):
                if i < taps:
                    first = (i * shards + shard) * count
                else:
                    first = (taps * shards + shard * (blocks - taps) + i - taps) * count
                block = total[first : first + count, low * half : (low + 1) * half]
                out_ref[to, :, i * half : (i + 1) * half] = block.astype(BF)


def plane_kernel(got_ref, out_ref):
    total = sum_of(got_ref).astype(BF)
    for z in range(out_ref.shape[0]):
        out_ref[z] = total


def rows_kernel(got_ref, conv_ref, expand_ref):
    count, width = conv_ref.shape[0], expand_ref.shape[1]
    half, taps = width // 2, conv_ref.shape[1] // width
    for low in range(2):
        total = got_ref[low].astype(F32)
        for z in range(low + 2, NZ, 2):
            total = total + got_ref[z].astype(F32)
        for i in range(got_ref.shape[2] // half):
            block = total[:, i * half : (i + 1) * half]
            if i < taps:
                conv_ref[:, i * width + low * half : i * width + (low + 1) * half] = block
            else:
                first = (i - taps) * count
                expand_ref[first : first + count, low * half : (low + 1) * half] = block


def in_vmem(array):
    return pltpu.with_memory_space_constraint(array, pltpu.VMEM)


def call(kernel, outs, *args, scratch=(), **options):
    return pl.pallas_call(
        kernel,
        out_shape=outs,
        scratch_shapes=list(scratch),
        compiler_params=VMEM_LIMIT,
        **options,
    )(*[in_vmem(a) for a in args])


def local(features, halting_map, grad_out, weight_reduce, weight_conv, weight_expand):
    samples, rows, cols, chans = features.shape
    width = weight_reduce.shape[0]
    taps = weight_conv.shape[1]
    own = samples * rows * cols
    inputs = (
        halting_map.reshape(samples * rows, 1, cols),
        features.reshape(own, chans),
        grad_out.reshape(own, chans),
        weight_reduce,
        weight_expand,
    )
    halting, flat_in, upstream, reduce_in, expand_in, hidden, sign, back, up, down = pl.pallas_call(
        enter_kernel,
        out_shape=[pltpu.VMEM(a.shape, a.dtype) for a in inputs]
        + [pltpu.VMEM((own, width), BF)] * 2
        + [pltpu.VMEM((2 * cols, width), BF)]
        + [pltpu.VMEM((3 * cols, width), BF)] * 2,
        in_specs=[pl.BlockSpec(memory_space=pl.ANY)] * len(inputs),
        scratch_shapes=[pltpu.SemaphoreType.DMA((len(inputs),))],
        compiler_params=VMEM_LIMIT,
    )(*[pltpu.with_memory_space_constraint(a, pltpu.MemorySpace.HBM) for a in inputs])
    from_prev = lax.ppermute(down, "rows", [(i, i + 1) for i in range(NZ - 1)])
    from_next = lax.ppermute(up, "rows", [(i + 1, i) for i in range(NZ - 1)])

    devices = NX * NY * NC
    conv_rows, expand_rows = width // devices, chans // devices
    shard_rows = conv_rows * taps // width + expand_rows
    part = (4, HX * HY * shard_rows, width)
    inner = (own - 2 * cols, width)
    conv_part, expand_part, two_in, gtwo_in = call(
        inner_kernel,
        [pltpu.VMEM((width, taps), F32), pltpu.VMEM((chans, width), F32), pltpu.VMEM(inner, BF), pltpu.VMEM(inner, BF)],
        halting, hidden, upstream, expand_in, weight_conv,
        scratch=[pltpu.VMEM((inner[0], taps), BF)],
    )
    keep, send, two, gtwo = call(
        outer_kernel,
        [pltpu.VMEM(part, BF), pltpu.VMEM(part, BF), pltpu.VMEM((2 * cols, width), BF), pltpu.VMEM((4 * cols, width), BF)],
        halting, hidden, back, from_prev, from_next, upstream, weight_conv, conv_part, expand_part,
        scratch=[pltpu.VMEM((4 * cols, taps), BF)],
    )

    got = lax.ppermute(send, "core", [(0, 1), (1, 0)])
    out, grad_in, done = call(
        functools.partial(leave_kernel, cols=cols),
        [jax.ShapeDtypeStruct((own, chans), BF)] * 2 + [pltpu.VMEM((8, 128), F32)],
        flat_in, upstream, two_in, two, gtwo_in, gtwo, sign, reduce_in, weight_conv, expand_in,
        scratch=[pltpu.VMEM((own, taps), BF), pltpu.VMEM((taps, width), BF)],
    )
    (total,) = call(core_kernel, [pltpu.VMEM(part, BF)], keep, got, done)
    got = lax.all_to_all(total, AXES, 0, 0, axis_index_groups=near_groups(), tiled=True)
    shard = (conv_rows, shard_rows // conv_rows * width // 2)
    (total,) = call(
        functools.partial(near_kernel, taps=taps // width), [pltpu.VMEM((2 * HX * HY,) + shard, BF)], got
    )
    got = lax.all_to_all(total, AXES, 0, 0, axis_index_groups=far_groups(), tiled=True)
    (total,) = call(plane_kernel, [pltpu.VMEM((NZ,) + shard, BF)], got)
    got = lax.all_to_all(total, "rows", 0, 0, tiled=True)
    grad_conv, grad_expand = call(
        rows_kernel,
        [jax.ShapeDtypeStruct((conv_rows, taps), F32), jax.ShapeDtypeStruct((expand_rows, width), F32)],
        got,
    )
    return (out.reshape(features.shape), grad_in.reshape(features.shape), grad_conv, grad_expand)


def solution(mesh):
    mesh = Mesh(mesh.devices.reshape(SIZES), AXES)
    whole = P(DP, "rows", None, None)
    in_specs = (whole, P(DP, "rows", None), whole, P(), P(), P())
    out_specs = (whole, whole, P(DP, None), P(DP, None))
    return jax.shard_map(local, mesh=mesh, in_specs=in_specs, out_specs=out_specs, check_vma=False)
```

```python
import functools

import jax
import jax.numpy as jnp
from jax import lax
from jax.experimental import pallas as pl
from jax.experimental.pallas import tpu as pltpu
from jax.sharding import Mesh, PartitionSpec as P

UNIT = 5
BF = jnp.bfloat16
F32 = jnp.float32

AXES = ("x_hi", "x_lo", "y_hi", "y_lo", "core", "rows")
SIZES = (2, 2, 4, 2, 2, 8)
DP = AXES[:5]
NX, NY, NC, NZ = 4, 8, 2, 8
HX, HY, HZ = NX // 2, NY // 2, NZ // 2
VMEM_LIMIT = pltpu.CompilerParams(vmem_limit_bytes=20 * 1024 * 1024)


def dp_of(x, y, core):
    return (x * NY + y) * NC + core


def near_groups():
    along_x = [
        [dp_of(x, y, 1) * NZ + z for x in range(NX)]
        for y in range(NY)
        for z in range(NZ)
    ]
    squares = [
        [dp_of(x, 2 * y_hi + i, 0) * NZ + 2 * z_hi + k for i in (0, 1) for k in (0, 1)]
        for x in range(NX)
        for y_hi in range(HY)
        for z_hi in range(HZ)
    ]
    return along_x + squares


def far_groups():
    columns = [
        [dp_of(x, y, 1) * NZ + 2 * z_hi + k for y in range(NY) for k in (0, 1)]
        for x in range(NX)
        for z_hi in range(HZ)
    ]
    planes = [
        [dp_of(x, 2 * y_hi + i, 0) * NZ + z for x in range(NX) for y_hi in range(HY)]
        for i in (0, 1)
        for z in range(NZ)
    ]
    return columns + planes


def dot(left, right, left_dim, right_dim):
    return lax.dot_general(
        left, right, (((left_dim,), (right_dim,)), ((), ())), preferred_element_type=F32
    )


def active_column(halt_ref, rows):
    cols = halt_ref.shape[2]
    at_row = lax.broadcasted_iota(jnp.int32, (cols, cols), 0)
    at_col = lax.broadcasted_iota(jnp.int32, (cols, cols), 1)
    parts = [
        jnp.sum(
            jnp.where((at_row == at_col) & (halt_ref[r] > UNIT), 1.0, 0.0), axis=1, keepdims=True
        )
        for r in rows
    ]
    return jnp.concatenate(parts, axis=0)


def neighbours(cells, cols):
    count = cells.shape[0]
    wide = cells.astype(F32)
    col = lax.broadcasted_iota(jnp.int32, (count, 1), 0) & (cols - 1)
    left = jnp.where(col == 0, 0.0, pltpu.roll(wide, 1, 0))
    right = jnp.where(col == cols - 1, 0.0, pltpu.roll(wide, count - 1, 0))
    return left.astype(BF), right.astype(BF)


def enter_kernel(
    halt_hbm, feat_hbm, grad_hbm, reduce_hbm, expand_hbm,
    halt_ref, feat_ref, grad_ref, reduce_ref, expand_ref,
    hidden_ref, sign_ref, back_ref, up_ref, down_ref, sems,
):
    pairs = (
        (feat_hbm, feat_ref),
        (reduce_hbm, reduce_ref),
        (halt_hbm, halt_ref),
        (grad_hbm, grad_ref),
        (expand_hbm, expand_ref),
    )
    copies = [pltpu.make_async_copy(src, dst, sems.at[i]) for i, (src, dst) in enumerate(pairs)]
    for copy in copies:
        copy.start()
    rows, _, cols = halt_ref.shape
    copies[0].wait()
    copies[1].wait()
    pre_one = dot(feat_ref[...], reduce_ref[...], 1, 1)
    hidden = jnp.maximum(pre_one, 0.0).astype(BF)
    hidden_ref[...] = hidden
    sign_ref[...] = (pre_one > 0).astype(F32).astype(BF)
    up_ref[0 : 2 * cols, :] = hidden[0 : 2 * cols]
    down_ref[0 : 2 * cols, :] = hidden[(rows - 2) * cols :]
    for copy in copies[2:]:
        copy.wait()
    edges = jnp.concatenate([grad_ref[0:cols, :], grad_ref[(rows - 1) * cols :, :]], axis=0)
    back = (active_column(halt_ref, (0, rows - 1)) * dot(edges, expand_ref[...], 1, 0)).astype(BF)
    back_ref[...] = back
    up_ref[2 * cols :, :] = back[0:cols]
    down_ref[2 * cols :, :] = back[cols:]


def fill_columns(columns_ref, first, cells, cols):
    width = cells.shape[1]
    count = cells.shape[0] - 2 * cols
    left, right = neighbours(cells, cols)
    for a in range(3):
        for b, shifted in enumerate((left, cells, right)):
            at = slice((3 * a + b) * width, (3 * a + b + 1) * width)
            columns_ref[first : first + count, at] = shifted[a * cols : a * cols + count]


def sorting(width):
    at = lax.broadcasted_iota(jnp.int32, (width, 1), 0)
    j, place, c = at & 3, (at >> 2) & (NX * NY - 1), at >> 7
    x, y = place >> 3, place & (NY - 1)
    other_x, other_y = (place >> 2) & (NX - 1), 2 * (place & (HY - 1)) + (place >> 4)
    wanted = jnp.where(c == 1, dp_of(x, y, 1), dp_of(other_x, other_y, 0)) * 4 + j
    channel = lax.broadcasted_iota(jnp.int32, (width, width), 1)
    return (channel == wanted).astype(F32).astype(BF)


def inner_kernel(
    halt_ref, hidden_ref, grad_ref, expand_ref, conv_ref,
    cpart_ref, epart_ref, two_ref, gtwo_ref, columns_ref,
):
    rows, _, cols = halt_ref.shape
    inner = slice(cols, (rows - 1) * cols)
    fill_columns(columns_ref, 0, hidden_ref[...], cols)
    pre_two = dot(columns_ref[...], conv_ref[...], 1, 1)
    back = active_column(halt_ref, range(1, rows - 1)) * dot(grad_ref[inner, :], expand_ref[...], 1, 0)
    grad_two = jnp.where(pre_two > 0, back, 0.0).astype(BF)
    gtwo_ref[...] = grad_two
    hidden_two = (active_column(halt_ref, range(1, rows - 1)) * jnp.maximum(pre_two, 0.0)).astype(BF)
    two_ref[...] = hidden_two
    grad_rows = dot(sorting(grad_two.shape[1]), grad_two, 1, 1).astype(BF)
    cpart_ref[...] = dot(grad_rows, columns_ref[...], 1, 0)
    epart_ref[...] = dot(grad_ref[inner, :], hidden_two, 0, 0)


def outer_kernel(
    halt_ref, hidden_ref, back_ref, next_ref, prev_ref, grad_ref, conv_ref, cpart_ref, epart_ref,
    keep_ref, send_ref, two_ref, gtwo_ref, columns_ref,
):
    rows, _, cols = halt_ref.shape
    width = hidden_ref.shape[1]
    core = lax.axis_index("core")
    top, end = slice(0, cols), slice((rows - 1) * cols, rows * cols)
    halo = 2 * cols
    above = jnp.concatenate([prev_ref[0:halo], hidden_ref[0:halo]], axis=0)
    below = jnp.concatenate([hidden_ref[(rows - 2) * cols :], next_ref[0:halo]], axis=0)
    fill_columns(columns_ref, 0, above, cols)
    fill_columns(columns_ref, halo, below, cols)
    pre_two = dot(columns_ref[...], conv_ref[...], 1, 1)
    back = jnp.concatenate([prev_ref[halo:], back_ref[...], next_ref[halo:]], axis=0)
    grad_two = jnp.where(pre_two > 0, back.astype(F32), 0.0).astype(BF)
    gtwo_ref[...] = grad_two
    active = active_column(halt_ref, (0, rows - 1))
    own = slice(cols, cols + halo)
    hidden_two = (active * jnp.maximum(pre_two[own], 0.0)).astype(BF)
    two_ref[...] = hidden_two

    grad_rows = dot(sorting(width), grad_two[own], 1, 1).astype(BF)
    conv_part = (cpart_ref[...] + dot(grad_rows, columns_ref[own, :], 1, 0)).astype(BF)
    upstream = jnp.concatenate([grad_ref[top, :], grad_ref[end, :]], axis=0)
    expand_part = (epart_ref[...] + dot(upstream, hidden_two, 0, 0)).astype(BF)

    def write(group, rows, low, along, square):
        at = slice(low * half, (low + 1) * half)
        keep_ref[group, rows, at] = jnp.where(core == 1, along, square)
        send_ref[group, rows, at] = jnp.where(core == 1, square, along)

    tall, taps, half = width // 8, conv_part.shape[1] // width, width // 2
    per_dp = expand_part.shape[0] // (NX * NY * NC)
    for group in range(4):
        y_lo, part = group // 2, group % 2
        for low in range(2):
            along = conv_part[(4 + group) * tall : (5 + group) * tall]
            first = (2 * y_lo + low) * tall
            square = conv_part[first : first + tall]
            for tap in range(taps):
                lanes = tap * width + low * half, tap * width + part * half
                rows = slice(tap * tall, (tap + 1) * tall)
                write(group, rows, low, along[:, lanes[0] : lanes[0] + half], square[:, lanes[1] : lanes[1] + half])
            for shard in range(NY):
                first = dp_of(group, shard, 1) * per_dp
                along_part = expand_part[first : first + per_dp, low * half : (low + 1) * half]
                first = dp_of(2 * low + shard // HY, 2 * (shard % HY) + y_lo, 0) * per_dp
                square_part = expand_part[first : first + per_dp, part * half : (part + 1) * half]
                start = taps * tall + shard * per_dp
                write(group, slice(start, start + per_dp), low, along_part, square_part)


def leave_kernel(
    feat_ref, grad_ref, two_in_ref, two_ref, gtwo_in_ref, gtwo_ref, sign_ref, reduce_ref, conv_ref, expand_ref,
    out_ref, gin_ref, done_ref, columns_ref, stacked_ref, *, cols,
):
    own = feat_ref.shape[0]
    width = two_ref.shape[1]
    two = jnp.concatenate([two_ref[0:cols], two_in_ref[...], two_ref[cols:]], axis=0)
    out_ref[...] = (feat_ref[...].astype(F32) + dot(two, expand_ref[...], 1, 1)).astype(BF)
    grad_two = jnp.concatenate([gtwo_ref[0 : 2 * cols], gtwo_in_ref[...], gtwo_ref[2 * cols :]], axis=0)
    left, right = neighbours(grad_two, cols)
    for a in range(3):
        for b, shifted in enumerate((right, grad_two, left)):
            tap = 3 * a + b
            at = slice(tap * width, (tap + 1) * width)
            columns_ref[:, at] = shifted[(2 - a) * cols : (2 - a) * cols + own]
            stacked_ref[at, :] = conv_ref[:, at]
    grad_hidden = dot(columns_ref[...], stacked_ref[...], 1, 0)
    grad_one = (grad_hidden * sign_ref[...].astype(F32)).astype(BF)
    gin_ref[...] = (grad_ref[...].astype(F32) + dot(grad_one, reduce_ref[...], 1, 0)).astype(BF)
    done_ref[...] = jnp.zeros_like(done_ref)


def sum_of(parts_ref):
    total = parts_ref[0].astype(F32)
    for i in range(1, parts_ref.shape[0]):
        total = total + parts_ref[i].astype(F32)
    return total


def core_kernel(keep_ref, got_ref, done_ref, out_ref):
    out_ref[...] = (keep_ref[...].astype(F32) + got_ref[...].astype(F32)).astype(BF)


def near_kernel(got_ref, out_ref, *, taps):
    total = sum_of(got_ref)
    core = lax.axis_index("core")
    parts, count, lanes = out_ref.shape
    half = total.shape[1] // 2
    shards, blocks = parts // 2, lanes // half
    for shard in range(shards):
        for low in range(2):
            to = jnp.where(core == 1, 2 * shard + low, shards * low + shard)
            for i in range(blocks):
                if i < taps:
                    first = (i * shards + shard) * count
                else:
                    first = (taps * shards + shard * (blocks - taps) + i - taps) * count
                block = total[first : first + count, low * half : (low + 1) * half]
                out_ref[to, :, i * half : (i + 1) * half] = block.astype(BF)


def plane_kernel(got_ref, out_ref):
    total = sum_of(got_ref).astype(BF)
    for z in range(out_ref.shape[0]):
        out_ref[z] = total


def rows_kernel(got_ref, conv_ref, expand_ref):
    count, width = conv_ref.shape[0], expand_ref.shape[1]
    half, taps = width // 2, conv_ref.shape[1] // width
    for low in range(2):
        total = got_ref[low].astype(F32)
        for z in range(low + 2, NZ, 2):
            total = total + got_ref[z].astype(F32)
        for i in range(got_ref.shape[2] // half):
            block = total[:, i * half : (i + 1) * half]
            if i < taps:
                conv_ref[:, i * width + low * half : i * width + (low + 1) * half] = block
            else:
                first = (i - taps) * count
                expand_ref[first : first + count, low * half : (low + 1) * half] = block


def in_vmem(array):
    return pltpu.with_memory_space_constraint(array, pltpu.VMEM)


def call(kernel, outs, *args, scratch=(), **options):
    return pl.pallas_call(
        kernel,
        out_shape=outs,
        scratch_shapes=list(scratch),
        compiler_params=VMEM_LIMIT,
        **options,
    )(*[in_vmem(a) for a in args])


def local(features, halting_map, grad_out, weight_reduce, weight_conv, weight_expand):
    samples, rows, cols, chans = features.shape
    width = weight_reduce.shape[0]
    taps = weight_conv.shape[1]
    own = samples * rows * cols
    inputs = (
        halting_map.reshape(samples * rows, 1, cols),
        features.reshape(own, chans),
        grad_out.reshape(own, chans),
        weight_reduce,
        weight_expand,
    )
    halting, flat_in, upstream, reduce_in, expand_in, hidden, sign, back, up, down = pl.pallas_call(
        enter_kernel,
        out_shape=[pltpu.VMEM(a.shape, a.dtype) for a in inputs]
        + [pltpu.VMEM((own, width), BF)] * 2
        + [pltpu.VMEM((2 * cols, width), BF)]
        + [pltpu.VMEM((3 * cols, width), BF)] * 2,
        in_specs=[pl.BlockSpec(memory_space=pl.ANY)] * len(inputs),
        scratch_shapes=[pltpu.SemaphoreType.DMA((len(inputs),))],
        compiler_params=VMEM_LIMIT,
    )(*[pltpu.with_memory_space_constraint(a, pltpu.MemorySpace.HBM) for a in inputs])
    from_next = lax.ppermute(up, "rows", [(i + 1, i) for i in range(NZ - 1)])
    from_prev = lax.ppermute(down, "rows", [(i, i + 1) for i in range(NZ - 1)])

    devices = NX * NY * NC
    conv_rows, expand_rows = width // devices, chans // devices
    shard_rows = conv_rows * taps // width + expand_rows
    part = (4, HX * HY * shard_rows, width)
    inner = (own - 2 * cols, width)
    conv_part, expand_part, two_in, gtwo_in = call(
        inner_kernel,
        [pltpu.VMEM((width, taps), F32), pltpu.VMEM((chans, width), F32), pltpu.VMEM(inner, BF), pltpu.VMEM(inner, BF)],
        halting, hidden, upstream, expand_in, weight_conv,
        scratch=[pltpu.VMEM((inner[0], taps), BF)],
    )
    keep, send, two, gtwo = call(
        outer_kernel,
        [pltpu.VMEM(part, BF), pltpu.VMEM(part, BF), pltpu.VMEM((2 * cols, width), BF), pltpu.VMEM((4 * cols, width), BF)],
        halting, hidden, back, from_next, from_prev, upstream, weight_conv, conv_part, expand_part,
        scratch=[pltpu.VMEM((4 * cols, taps), BF)],
    )

    got = lax.ppermute(send, "core", [(0, 1), (1, 0)])
    out, grad_in, done = call(
        functools.partial(leave_kernel, cols=cols),
        [jax.ShapeDtypeStruct((own, chans), BF)] * 2 + [pltpu.VMEM((8, 128), F32)],
        flat_in, upstream, two_in, two, gtwo_in, gtwo, sign, reduce_in, weight_conv, expand_in,
        scratch=[pltpu.VMEM((own, taps), BF), pltpu.VMEM((taps, width), BF)],
    )
    (total,) = call(core_kernel, [pltpu.VMEM(part, BF)], keep, got, done)
    got = lax.all_to_all(total, AXES, 0, 0, axis_index_groups=near_groups(), tiled=True)
    shard = (conv_rows, shard_rows // conv_rows * width // 2)
    (total,) = call(
        functools.partial(near_kernel, taps=taps // width), [pltpu.VMEM((2 * HX * HY,) + shard, BF)], got
    )
    got = lax.all_to_all(total, AXES, 0, 0, axis_index_groups=far_groups(), tiled=True)
    (total,) = call(plane_kernel, [pltpu.VMEM((NZ,) + shard, BF)], got)
    got = lax.all_to_all(total, "rows", 0, 0, tiled=True)
    grad_conv, grad_expand = call(
        rows_kernel,
        [jax.ShapeDtypeStruct((conv_rows, taps), F32), jax.ShapeDtypeStruct((expand_rows, width), F32)],
        got,
    )
    return (out.reshape(features.shape), grad_in.reshape(features.shape), grad_conv, grad_expand)


def solution(mesh):
    mesh = Mesh(mesh.devices.reshape(SIZES), AXES)
    whole = P(DP, "rows", None, None)
    in_specs = (whole, P(DP, "rows", None), whole, P(), P(), P())
    out_specs = (whole, whole, P(DP, None), P(DP, None))
    return jax.shard_map(local, mesh=mesh, in_specs=in_specs, out_specs=out_specs, check_vma=False)
```

```python
import functools

import jax
import jax.numpy as jnp
from jax import lax
from jax.experimental import pallas as pl
from jax.experimental.pallas import tpu as pltpu
from jax.sharding import Mesh, PartitionSpec as P

UNIT = 5
BF = jnp.bfloat16
F32 = jnp.float32

AXES = ("x_hi", "x_lo", "y_hi", "y_lo", "core", "rows")
SIZES = (2, 2, 4, 2, 2, 8)
DP = AXES[:5]
NX, NY, NC, NZ = 4, 8, 2, 8
HX, HY, HZ = NX // 2, NY // 2, NZ // 2
VMEM_LIMIT = pltpu.CompilerParams(vmem_limit_bytes=20 * 1024 * 1024)


def dp_of(x, y, core):
    return (x * NY + y) * NC + core


def near_groups():
    along_x = [
        [dp_of(x, y, 1) * NZ + z for x in range(NX)]
        for y in range(NY)
        for z in range(NZ)
    ]
    squares = [
        [dp_of(x, 2 * y_hi + i, 0) * NZ + 2 * z_hi + k for i in (0, 1) for k in (0, 1)]
        for x in range(NX)
        for y_hi in range(HY)
        for z_hi in range(HZ)
    ]
    return along_x + squares


def far_groups():
    columns = [
        [dp_of(x, y, 1) * NZ + 2 * z_hi + k for y in range(NY) for k in (0, 1)]
        for x in range(NX)
        for z_hi in range(HZ)
    ]
    planes = [
        [dp_of(x, 2 * y_hi + i, 0) * NZ + z for x in range(NX) for y_hi in range(HY)]
        for i in (0, 1)
        for z in range(NZ)
    ]
    return columns + planes


def dot(left, right, left_dim, right_dim):
    return lax.dot_general(
        left, right, (((left_dim,), (right_dim,)), ((), ())), preferred_element_type=F32
    )


def active_column(halt_ref, rows):
    cols = halt_ref.shape[2]
    at_row = lax.broadcasted_iota(jnp.int32, (cols, cols), 0)
    at_col = lax.broadcasted_iota(jnp.int32, (cols, cols), 1)
    parts = [
        jnp.sum(
            jnp.where((at_row == at_col) & (halt_ref[r] > UNIT), 1.0, 0.0), axis=1, keepdims=True
        )
        for r in rows
    ]
    return jnp.concatenate(parts, axis=0)


def neighbours(cells, cols):
    count = cells.shape[0]
    wide = cells.astype(F32)
    col = lax.broadcasted_iota(jnp.int32, (count, 1), 0) & (cols - 1)
    left = jnp.where(col == 0, 0.0, pltpu.roll(wide, 1, 0))
    right = jnp.where(col == cols - 1, 0.0, pltpu.roll(wide, count - 1, 0))
    return left.astype(BF), right.astype(BF)


def enter_kernel(
    halt_hbm, feat_hbm, grad_hbm, reduce_hbm, expand_hbm,
    halt_ref, feat_ref, grad_ref, reduce_ref, expand_ref,
    hidden_ref, sign_ref, back_ref, up_ref, down_ref, sems,
):
    pairs = (
        (feat_hbm, feat_ref),
        (reduce_hbm, reduce_ref),
        (halt_hbm, halt_ref),
        (grad_hbm, grad_ref),
        (expand_hbm, expand_ref),
    )
    copies = [pltpu.make_async_copy(src, dst, sems.at[i]) for i, (src, dst) in enumerate(pairs)]
    for copy in copies:
        copy.start()
    rows, _, cols = halt_ref.shape
    copies[0].wait()
    copies[1].wait()
    pre_one = dot(feat_ref[...], reduce_ref[...], 1, 1)
    hidden = jnp.maximum(pre_one, 0.0).astype(BF)
    hidden_ref[...] = hidden
    sign_ref[...] = (pre_one > 0).astype(F32).astype(BF)
    up_ref[0 : 2 * cols, :] = hidden[0 : 2 * cols]
    down_ref[0 : 2 * cols, :] = hidden[(rows - 2) * cols :]
    for copy in copies[2:]:
        copy.wait()
    edges = jnp.concatenate([grad_ref[0:cols, :], grad_ref[(rows - 1) * cols :, :]], axis=0)
    back = (active_column(halt_ref, (0, rows - 1)) * dot(edges, expand_ref[...], 1, 0)).astype(BF)
    back_ref[...] = back
    up_ref[2 * cols :, :] = back[0:cols]
    down_ref[2 * cols :, :] = back[cols:]


def fill_columns(columns_ref, first, cells, cols):
    width = cells.shape[1]
    count = cells.shape[0] - 2 * cols
    left, right = neighbours(cells, cols)
    for a in range(3):
        for b, shifted in enumerate((left, cells, right)):
            at = slice((3 * a + b) * width, (3 * a + b + 1) * width)
            columns_ref[first : first + count, at] = shifted[a * cols : a * cols + count]


def sorting(width):
    at = lax.broadcasted_iota(jnp.int32, (width, 1), 0)
    j, place, c = at & 3, (at >> 2) & (NX * NY - 1), at >> 7
    x, y = place >> 3, place & (NY - 1)
    other_x, other_y = (place >> 2) & (NX - 1), 2 * (place & (HY - 1)) + (place >> 4)
    wanted = jnp.where(c == 1, dp_of(x, y, 1), dp_of(other_x, other_y, 0)) * 4 + j
    channel = lax.broadcasted_iota(jnp.int32, (width, width), 1)
    return (channel == wanted).astype(F32).astype(BF)


def inner_kernel(
    halt_ref, hidden_ref, grad_ref, expand_ref, conv_ref,
    cpart_ref, epart_ref, two_ref, gtwo_ref, columns_ref,
):
    rows, _, cols = halt_ref.shape
    inner = slice(cols, (rows - 1) * cols)
    fill_columns(columns_ref, 0, hidden_ref[...], cols)
    pre_two = dot(columns_ref[...], conv_ref[...], 1, 1)
    back = active_column(halt_ref, range(1, rows - 1)) * dot(grad_ref[inner, :], expand_ref[...], 1, 0)
    grad_two = jnp.where(pre_two > 0, back, 0.0).astype(BF)
    gtwo_ref[...] = grad_two
    hidden_two = (active_column(halt_ref, range(1, rows - 1)) * jnp.maximum(pre_two, 0.0)).astype(BF)
    two_ref[...] = hidden_two
    grad_rows = dot(sorting(grad_two.shape[1]), grad_two, 1, 1).astype(BF)
    cpart_ref[...] = dot(grad_rows, columns_ref[...], 1, 0)
    epart_ref[...] = dot(grad_ref[inner, :], hidden_two, 0, 0)


def outer_kernel(
    halt_ref, hidden_ref, back_ref, next_ref, prev_ref, grad_ref, conv_ref, cpart_ref, epart_ref,
    keep_ref, send_ref, two_ref, gtwo_ref, columns_ref,
):
    rows, _, cols = halt_ref.shape
    width = hidden_ref.shape[1]
    core = lax.axis_index("core")
    top, end = slice(0, cols), slice((rows - 1) * cols, rows * cols)
    halo = 2 * cols
    above = jnp.concatenate([prev_ref[0:halo], hidden_ref[0:halo]], axis=0)
    below = jnp.concatenate([hidden_ref[(rows - 2) * cols :], next_ref[0:halo]], axis=0)
    fill_columns(columns_ref, 0, above, cols)
    fill_columns(columns_ref, halo, below, cols)
    pre_two = dot(columns_ref[...], conv_ref[...], 1, 1)
    back = jnp.concatenate([prev_ref[halo:], back_ref[...], next_ref[halo:]], axis=0)
    grad_two = jnp.where(pre_two > 0, back.astype(F32), 0.0).astype(BF)
    gtwo_ref[...] = grad_two
    active = active_column(halt_ref, (0, rows - 1))
    own = slice(cols, cols + halo)
    hidden_two = (active * jnp.maximum(pre_two[own], 0.0)).astype(BF)
    two_ref[...] = hidden_two

    grad_rows = dot(sorting(width), grad_two[own], 1, 1).astype(BF)
    conv_part = (cpart_ref[...] + dot(grad_rows, columns_ref[own, :], 1, 0)).astype(BF)
    upstream = jnp.concatenate([grad_ref[top, :], grad_ref[end, :]], axis=0)
    expand_part = (epart_ref[...] + dot(upstream, hidden_two, 0, 0)).astype(BF)

    def write(group, rows, low, along, square):
        at = slice(low * half, (low + 1) * half)
        keep_ref[group, rows, at] = jnp.where(core == 1, along, square)
        send_ref[group, rows, at] = jnp.where(core == 1, square, along)

    tall, taps, half = width // 8, conv_part.shape[1] // width, width // 2
    per_dp = expand_part.shape[0] // (NX * NY * NC)
    for group in range(4):
        y_lo, part = group // 2, group % 2
        for low in range(2):
            along = conv_part[(4 + group) * tall : (5 + group) * tall]
            first = (2 * y_lo + low) * tall
            square = conv_part[first : first + tall]
            for tap in range(taps):
                lanes = tap * width + low * half, tap * width + part * half
                rows = slice(tap * tall, (tap + 1) * tall)
                write(group, rows, low, along[:, lanes[0] : lanes[0] + half], square[:, lanes[1] : lanes[1] + half])
            for shard in range(NY):
                first = dp_of(group, shard, 1) * per_dp
                along_part = expand_part[first : first + per_dp, low * half : (low + 1) * half]
                first = dp_of(2 * low + shard // HY, 2 * (shard % HY) + y_lo, 0) * per_dp
                square_part = expand_part[first : first + per_dp, part * half : (part + 1) * half]
                start = taps * tall + shard * per_dp
                write(group, slice(start, start + per_dp), low, along_part, square_part)


def leave_kernel(
    feat_ref, grad_ref, two_in_ref, two_ref, gtwo_in_ref, gtwo_ref, sign_ref, reduce_ref, conv_ref, expand_ref,
    out_ref, gin_ref, done_ref, columns_ref, stacked_ref, out_buf, gin_buf, sems, *, cols,
):
    own = feat_ref.shape[0]
    width = two_ref.shape[1]
    two = jnp.concatenate([two_ref[0:cols], two_in_ref[...], two_ref[cols:]], axis=0)
    out_buf[...] = (feat_ref[...].astype(F32) + dot(two, expand_ref[...], 1, 1)).astype(BF)
    copies = [pltpu.make_async_copy(out_buf, out_ref, sems.at[0])]
    copies[0].start()
    grad_two = jnp.concatenate([gtwo_ref[0 : 2 * cols], gtwo_in_ref[...], gtwo_ref[2 * cols :]], axis=0)
    left, right = neighbours(grad_two, cols)
    for a in range(3):
        for b, shifted in enumerate((right, grad_two, left)):
            tap = 3 * a + b
            at = slice(tap * width, (tap + 1) * width)
            columns_ref[:, at] = shifted[(2 - a) * cols : (2 - a) * cols + own]
            stacked_ref[at, :] = conv_ref[:, at]
    grad_hidden = dot(columns_ref[...], stacked_ref[...], 1, 0)
    grad_one = (grad_hidden * sign_ref[...].astype(F32)).astype(BF)
    half = own // 2
    for i in range(2):
        at = pl.ds(i * half, half)
        back = dot(grad_one[i * half : (i + 1) * half], reduce_ref[...], 1, 0)
        gin_buf[at, :] = (grad_ref[at, :].astype(F32) + back).astype(BF)
        copies.append(pltpu.make_async_copy(gin_buf.at[at], gin_ref.at[at], sems.at[1 + i]))
        copies[-1].start()
    done_ref[...] = jnp.zeros_like(done_ref)
    for copy in copies:
        copy.wait()


def sum_of(parts_ref):
    total = parts_ref[0].astype(F32)
    for i in range(1, parts_ref.shape[0]):
        total = total + parts_ref[i].astype(F32)
    return total


def core_kernel(keep_ref, got_ref, done_ref, out_ref):
    out_ref[...] = (keep_ref[...].astype(F32) + got_ref[...].astype(F32)).astype(BF)


def near_kernel(got_ref, out_ref, *, taps):
    total = sum_of(got_ref)
    core = lax.axis_index("core")
    parts, count, lanes = out_ref.shape
    half = total.shape[1] // 2
    shards, blocks = parts // 2, lanes // half
    for shard in range(shards):
        for low in range(2):
            to = jnp.where(core == 1, 2 * shard + low, shards * low + shard)
            for i in range(blocks):
                if i < taps:
                    first = (i * shards + shard) * count
                else:
                    first = (taps * shards + shard * (blocks - taps) + i - taps) * count
                block = total[first : first + count, low * half : (low + 1) * half]
                out_ref[to, :, i * half : (i + 1) * half] = block.astype(BF)


def plane_kernel(got_ref, out_ref):
    total = sum_of(got_ref).astype(BF)
    for z in range(out_ref.shape[0]):
        out_ref[z] = total


def rows_kernel(got_ref, conv_ref, expand_ref):
    count, width = conv_ref.shape[0], expand_ref.shape[1]
    half, taps = width // 2, conv_ref.shape[1] // width
    for low in range(2):
        total = got_ref[low].astype(F32)
        for z in range(low + 2, NZ, 2):
            total = total + got_ref[z].astype(F32)
        for i in range(got_ref.shape[2] // half):
            block = total[:, i * half : (i + 1) * half]
            if i < taps:
                conv_ref[:, i * width + low * half : i * width + (low + 1) * half] = block
            else:
                first = (i - taps) * count
                expand_ref[first : first + count, low * half : (low + 1) * half] = block


def in_vmem(array):
    return pltpu.with_memory_space_constraint(array, pltpu.VMEM)


def call(kernel, outs, *args, scratch=(), **options):
    return pl.pallas_call(
        kernel,
        out_shape=outs,
        scratch_shapes=list(scratch),
        compiler_params=VMEM_LIMIT,
        **options,
    )(*[in_vmem(a) for a in args])


def local(features, halting_map, grad_out, weight_reduce, weight_conv, weight_expand):
    samples, rows, cols, chans = features.shape
    width = weight_reduce.shape[0]
    taps = weight_conv.shape[1]
    own = samples * rows * cols
    inputs = (
        halting_map.reshape(samples * rows, 1, cols),
        features.reshape(own, chans),
        grad_out.reshape(own, chans),
        weight_reduce,
        weight_expand,
    )
    halting, flat_in, upstream, reduce_in, expand_in, hidden, sign, back, up, down = pl.pallas_call(
        enter_kernel,
        out_shape=[pltpu.VMEM(a.shape, a.dtype) for a in inputs]
        + [pltpu.VMEM((own, width), BF)] * 2
        + [pltpu.VMEM((2 * cols, width), BF)]
        + [pltpu.VMEM((3 * cols, width), BF)] * 2,
        in_specs=[pl.BlockSpec(memory_space=pl.ANY)] * len(inputs),
        scratch_shapes=[pltpu.SemaphoreType.DMA((len(inputs),))],
        compiler_params=VMEM_LIMIT,
    )(*[pltpu.with_memory_space_constraint(a, pltpu.MemorySpace.HBM) for a in inputs])
    from_next = lax.ppermute(up, "rows", [(i + 1, i) for i in range(NZ - 1)])
    from_prev = lax.ppermute(down, "rows", [(i, i + 1) for i in range(NZ - 1)])

    devices = NX * NY * NC
    conv_rows, expand_rows = width // devices, chans // devices
    shard_rows = conv_rows * taps // width + expand_rows
    part = (4, HX * HY * shard_rows, width)
    inner = (own - 2 * cols, width)
    conv_part, expand_part, two_in, gtwo_in = call(
        inner_kernel,
        [pltpu.VMEM((width, taps), F32), pltpu.VMEM((chans, width), F32), pltpu.VMEM(inner, BF), pltpu.VMEM(inner, BF)],
        halting, hidden, upstream, expand_in, weight_conv,
        scratch=[pltpu.VMEM((inner[0], taps), BF)],
    )
    keep, send, two, gtwo = call(
        outer_kernel,
        [pltpu.VMEM(part, BF), pltpu.VMEM(part, BF), pltpu.VMEM((2 * cols, width), BF), pltpu.VMEM((4 * cols, width), BF)],
        halting, hidden, back, from_next, from_prev, upstream, weight_conv, conv_part, expand_part,
        scratch=[pltpu.VMEM((4 * cols, taps), BF)],
    )

    got = lax.ppermute(send, "core", [(0, 1), (1, 0)])
    out, grad_in, done = call(
        functools.partial(leave_kernel, cols=cols),
        [jax.ShapeDtypeStruct((own, chans), BF)] * 2 + [pltpu.VMEM((8, 128), F32)],
        flat_in, upstream, two_in, two, gtwo_in, gtwo, sign, reduce_in, weight_conv, expand_in,
        scratch=[
            pltpu.VMEM((own, taps), BF),
            pltpu.VMEM((taps, width), BF),
            pltpu.VMEM((own, chans), BF),
            pltpu.VMEM((own, chans), BF),
            pltpu.SemaphoreType.DMA((3,)),
        ],
        out_specs=[pl.BlockSpec(memory_space=pl.ANY)] * 2 + [pl.BlockSpec(memory_space=pltpu.VMEM)],
    )
    (total,) = call(core_kernel, [pltpu.VMEM(part, BF)], keep, got, done)
    got = lax.all_to_all(total, AXES, 0, 0, axis_index_groups=near_groups(), tiled=True)
    shard = (conv_rows, shard_rows // conv_rows * width // 2)
    (total,) = call(
        functools.partial(near_kernel, taps=taps // width), [pltpu.VMEM((2 * HX * HY,) + shard, BF)], got
    )
    got = lax.all_to_all(total, AXES, 0, 0, axis_index_groups=far_groups(), tiled=True)
    (total,) = call(plane_kernel, [pltpu.VMEM((NZ,) + shard, BF)], got)
    got = lax.all_to_all(total, "rows", 0, 0, tiled=True)
    grad_conv, grad_expand = call(
        rows_kernel,
        [jax.ShapeDtypeStruct((conv_rows, taps), F32), jax.ShapeDtypeStruct((expand_rows, width), F32)],
        got,
    )
    return (out.reshape(features.shape), grad_in.reshape(features.shape), grad_conv, grad_expand)


def solution(mesh):
    mesh = Mesh(mesh.devices.reshape(SIZES), AXES)
    whole = P(DP, "rows", None, None)
    in_specs = (whole, P(DP, "rows", None), whole, P(), P(), P())
    out_specs = (whole, whole, P(DP, None), P(DP, None))
    return jax.shard_map(local, mesh=mesh, in_specs=in_specs, out_specs=out_specs, check_vma=False)
```

```python
import functools

import jax
import jax.numpy as jnp
from jax import lax
from jax.experimental import pallas as pl
from jax.experimental.pallas import tpu as pltpu
from jax.sharding import Mesh, PartitionSpec as P

UNIT = 5
BF = jnp.bfloat16
F32 = jnp.float32

AXES = ("x_hi", "x_lo", "y_hi", "y_lo", "core", "rows")
SIZES = (2, 2, 4, 2, 2, 8)
DP = AXES[:5]
NX, NY, NC, NZ = 4, 8, 2, 8
HX, HY, HZ = NX // 2, NY // 2, NZ // 2
VMEM_LIMIT = pltpu.CompilerParams(vmem_limit_bytes=20 * 1024 * 1024)


def dp_of(x, y, core):
    return (x * NY + y) * NC + core


def near_groups():
    along_x = [
        [dp_of(x, y, 1) * NZ + z for x in range(NX)]
        for y in range(NY)
        for z in range(NZ)
    ]
    squares = [
        [dp_of(x, 2 * y_hi + i, 0) * NZ + 2 * z_hi + k for i in (0, 1) for k in (0, 1)]
        for x in range(NX)
        for y_hi in range(HY)
        for z_hi in range(HZ)
    ]
    return along_x + squares


def far_groups():
    columns = [
        [dp_of(x, y, 1) * NZ + 2 * z_hi + k for y in range(NY) for k in (0, 1)]
        for x in range(NX)
        for z_hi in range(HZ)
    ]
    planes = [
        [dp_of(x, 2 * y_hi + i, 0) * NZ + z for x in range(NX) for y_hi in range(HY)]
        for i in (0, 1)
        for z in range(NZ)
    ]
    return columns + planes


def dot(left, right, left_dim, right_dim):
    return lax.dot_general(
        left, right, (((left_dim,), (right_dim,)), ((), ())), preferred_element_type=F32
    )


def active_column(halt_ref, rows):
    cols = halt_ref.shape[2]
    at_row = lax.broadcasted_iota(jnp.int32, (cols, cols), 0)
    at_col = lax.broadcasted_iota(jnp.int32, (cols, cols), 1)
    parts = [
        jnp.sum(
            jnp.where((at_row == at_col) & (halt_ref[r] > UNIT), 1.0, 0.0), axis=1, keepdims=True
        )
        for r in rows
    ]
    return jnp.concatenate(parts, axis=0)


def neighbours(cells, cols):
    count = cells.shape[0]
    wide = cells.astype(F32)
    col = lax.broadcasted_iota(jnp.int32, (count, 1), 0) & (cols - 1)
    left = jnp.where(col == 0, 0.0, pltpu.roll(wide, 1, 0))
    right = jnp.where(col == cols - 1, 0.0, pltpu.roll(wide, count - 1, 0))
    return left.astype(BF), right.astype(BF)


def enter_kernel(
    halt_hbm, feat_hbm, grad_hbm, reduce_hbm, expand_hbm,
    halt_ref, feat_ref, grad_ref, reduce_ref, expand_ref,
    hidden_ref, sign_ref, back_ref, up_ref, down_ref, sems,
):
    pairs = (
        (feat_hbm, feat_ref),
        (reduce_hbm, reduce_ref),
        (halt_hbm, halt_ref),
        (grad_hbm, grad_ref),
        (expand_hbm, expand_ref),
    )
    copies = [pltpu.make_async_copy(src, dst, sems.at[i]) for i, (src, dst) in enumerate(pairs)]
    for copy in copies:
        copy.start()
    rows, _, cols = halt_ref.shape
    copies[0].wait()
    copies[1].wait()
    pre_one = dot(feat_ref[...], reduce_ref[...], 1, 1)
    hidden = jnp.maximum(pre_one, 0.0).astype(BF)
    hidden_ref[...] = hidden
    sign_ref[...] = (pre_one > 0).astype(F32).astype(BF)
    up_ref[0 : 2 * cols, :] = hidden[0 : 2 * cols]
    down_ref[0 : 2 * cols, :] = hidden[(rows - 2) * cols :]
    for copy in copies[2:]:
        copy.wait()
    edges = jnp.concatenate([grad_ref[0:cols, :], grad_ref[(rows - 1) * cols :, :]], axis=0)
    back = (active_column(halt_ref, (0, rows - 1)) * dot(edges, expand_ref[...], 1, 0)).astype(BF)
    back_ref[...] = back
    up_ref[2 * cols :, :] = back[0:cols]
    down_ref[2 * cols :, :] = back[cols:]


def fill_columns(columns_ref, first, cells, cols):
    width = cells.shape[1]
    count = cells.shape[0] - 2 * cols
    left, right = neighbours(cells, cols)
    for a in range(3):
        for b, shifted in enumerate((left, cells, right)):
            at = slice((3 * a + b) * width, (3 * a + b + 1) * width)
            columns_ref[first : first + count, at] = shifted[a * cols : a * cols + count]


def sorting(width):
    at = lax.broadcasted_iota(jnp.int32, (width, 1), 0)
    j, place, c = at & 3, (at >> 2) & (NX * NY - 1), at >> 7
    x, y = place >> 3, place & (NY - 1)
    other_x, other_y = (place >> 2) & (NX - 1), 2 * (place & (HY - 1)) + (place >> 4)
    wanted = jnp.where(c == 1, dp_of(x, y, 1), dp_of(other_x, other_y, 0)) * 4 + j
    channel = lax.broadcasted_iota(jnp.int32, (width, width), 1)
    return (channel == wanted).astype(F32).astype(BF)


def inner_kernel(
    halt_ref, hidden_ref, back_ref, next_ref, grad_ref, expand_ref, conv_ref,
    cpart_ref, epart_ref, two_ref, gtwo_ref, columns_ref,
):
    rows, _, cols = halt_ref.shape
    mine, middle = slice(cols, rows * cols), (rows - 2) * cols
    own = slice(0, (rows - 1) * cols)
    fill_columns(columns_ref, 0, jnp.concatenate([hidden_ref[...], next_ref[0 : 2 * cols]], axis=0), cols)
    pre_two = dot(columns_ref[...], conv_ref[...], 1, 1)
    active = active_column(halt_ref, range(1, rows))
    back = (active[0:middle] * dot(grad_ref[cols : cols + middle, :], expand_ref[...], 1, 0)).astype(BF)
    back = jnp.concatenate([back, back_ref[cols:], next_ref[2 * cols :]], axis=0)
    grad_two = jnp.where(pre_two > 0, back.astype(F32), 0.0).astype(BF)
    gtwo_ref[...] = grad_two
    hidden_two = (active * jnp.maximum(pre_two[own], 0.0)).astype(BF)
    two_ref[...] = hidden_two
    grad_rows = dot(sorting(grad_two.shape[1]), grad_two[own], 1, 1).astype(BF)
    cpart_ref[...] = dot(grad_rows, columns_ref[own, :], 1, 0)
    epart_ref[...] = dot(grad_ref[mine, :], hidden_two, 0, 0)


def outer_kernel(
    halt_ref, hidden_ref, back_ref, prev_ref, grad_ref, conv_ref, cpart_ref, epart_ref,
    keep_ref, send_ref, two_ref, gtwo_ref, columns_ref,
):
    cols = halt_ref.shape[2]
    width = hidden_ref.shape[1]
    core = lax.axis_index("core")
    halo = 2 * cols
    above = jnp.concatenate([prev_ref[0:halo], hidden_ref[0:halo]], axis=0)
    fill_columns(columns_ref, 0, above, cols)
    pre_two = dot(columns_ref[...], conv_ref[...], 1, 1)
    back = jnp.concatenate([prev_ref[halo:], back_ref[0:cols]], axis=0)
    grad_two = jnp.where(pre_two > 0, back.astype(F32), 0.0).astype(BF)
    gtwo_ref[...] = grad_two
    active = active_column(halt_ref, (0,))
    own = slice(cols, halo)
    hidden_two = (active * jnp.maximum(pre_two[own], 0.0)).astype(BF)
    two_ref[...] = hidden_two

    grad_rows = dot(sorting(width), grad_two[own], 1, 1).astype(BF)
    conv_part = (cpart_ref[...] + dot(grad_rows, columns_ref[own, :], 1, 0)).astype(BF)
    upstream = grad_ref[0:cols, :]
    expand_part = (epart_ref[...] + dot(upstream, hidden_two, 0, 0)).astype(BF)

    def write(group, rows, low, along, square):
        at = slice(low * half, (low + 1) * half)
        keep_ref[group, rows, at] = jnp.where(core == 1, along, square)
        send_ref[group, rows, at] = jnp.where(core == 1, square, along)

    tall, taps, half = width // 8, conv_part.shape[1] // width, width // 2
    per_dp = expand_part.shape[0] // (NX * NY * NC)
    for group in range(4):
        y_lo, part = group // 2, group % 2
        for low in range(2):
            along = conv_part[(4 + group) * tall : (5 + group) * tall]
            first = (2 * y_lo + low) * tall
            square = conv_part[first : first + tall]
            for tap in range(taps):
                lanes = tap * width + low * half, tap * width + part * half
                rows = slice(tap * tall, (tap + 1) * tall)
                write(group, rows, low, along[:, lanes[0] : lanes[0] + half], square[:, lanes[1] : lanes[1] + half])
            for shard in range(NY):
                first = dp_of(group, shard, 1) * per_dp
                along_part = expand_part[first : first + per_dp, low * half : (low + 1) * half]
                first = dp_of(2 * low + shard // HY, 2 * (shard % HY) + y_lo, 0) * per_dp
                square_part = expand_part[first : first + per_dp, part * half : (part + 1) * half]
                start = taps * tall + shard * per_dp
                write(group, slice(start, start + per_dp), low, along_part, square_part)


def leave_kernel(
    feat_ref, grad_ref, two_in_ref, two_ref, gtwo_in_ref, gtwo_ref, sign_ref, reduce_ref, conv_ref, expand_ref,
    out_ref, gin_ref, done_ref, columns_ref, stacked_ref, *, cols,
):
    own = feat_ref.shape[0]
    width = two_ref.shape[1]
    two = jnp.concatenate([two_ref[...], two_in_ref[...]], axis=0)
    out_ref[...] = (feat_ref[...].astype(F32) + dot(two, expand_ref[...], 1, 1)).astype(BF)
    grad_two = jnp.concatenate([gtwo_ref[...], gtwo_in_ref[...]], axis=0)
    left, right = neighbours(grad_two, cols)
    for a in range(3):
        for b, shifted in enumerate((right, grad_two, left)):
            tap = 3 * a + b
            at = slice(tap * width, (tap + 1) * width)
            columns_ref[:, at] = shifted[(2 - a) * cols : (2 - a) * cols + own]
            stacked_ref[at, :] = conv_ref[:, at]
    grad_hidden = dot(columns_ref[...], stacked_ref[...], 1, 0)
    grad_one = (grad_hidden * sign_ref[...].astype(F32)).astype(BF)
    gin_ref[...] = (grad_ref[...].astype(F32) + dot(grad_one, reduce_ref[...], 1, 0)).astype(BF)
    done_ref[...] = jnp.zeros_like(done_ref)


def sum_of(parts_ref):
    total = parts_ref[0].astype(F32)
    for i in range(1, parts_ref.shape[0]):
        total = total + parts_ref[i].astype(F32)
    return total


def core_kernel(keep_ref, got_ref, done_ref, out_ref):
    out_ref[...] = (keep_ref[...].astype(F32) + got_ref[...].astype(F32)).astype(BF)


def near_kernel(got_ref, out_ref, *, taps):
    total = sum_of(got_ref)
    core = lax.axis_index("core")
    parts, count, lanes = out_ref.shape
    half = total.shape[1] // 2
    shards, blocks = parts // 2, lanes // half
    for shard in range(shards):
        for low in range(2):
            to = jnp.where(core == 1, 2 * shard + low, shards * low + shard)
            for i in range(blocks):
                if i < taps:
                    first = (i * shards + shard) * count
                else:
                    first = (taps * shards + shard * (blocks - taps) + i - taps) * count
                block = total[first : first + count, low * half : (low + 1) * half]
                out_ref[to, :, i * half : (i + 1) * half] = block.astype(BF)


def plane_kernel(got_ref, out_ref):
    total = sum_of(got_ref).astype(BF)
    for z in range(out_ref.shape[0]):
        out_ref[z] = total


def rows_kernel(got_ref, conv_ref, expand_ref):
    count, width = conv_ref.shape[0], expand_ref.shape[1]
    half, taps = width // 2, conv_ref.shape[1] // width
    for low in range(2):
        total = got_ref[low].astype(F32)
        for z in range(low + 2, NZ, 2):
            total = total + got_ref[z].astype(F32)
        for i in range(got_ref.shape[2] // half):
            block = total[:, i * half : (i + 1) * half]
            if i < taps:
                conv_ref[:, i * width + low * half : i * width + (low + 1) * half] = block
            else:
                first = (i - taps) * count
                expand_ref[first : first + count, low * half : (low + 1) * half] = block


def in_vmem(array):
    return pltpu.with_memory_space_constraint(array, pltpu.VMEM)


def call(kernel, outs, *args, scratch=(), **options):
    return pl.pallas_call(
        kernel,
        out_shape=outs,
        scratch_shapes=list(scratch),
        compiler_params=VMEM_LIMIT,
        **options,
    )(*[in_vmem(a) for a in args])


def local(features, halting_map, grad_out, weight_reduce, weight_conv, weight_expand):
    samples, rows, cols, chans = features.shape
    width = weight_reduce.shape[0]
    taps = weight_conv.shape[1]
    own = samples * rows * cols
    inputs = (
        halting_map.reshape(samples * rows, 1, cols),
        features.reshape(own, chans),
        grad_out.reshape(own, chans),
        weight_reduce,
        weight_expand,
    )
    halting, flat_in, upstream, reduce_in, expand_in, hidden, sign, back, up, down = pl.pallas_call(
        enter_kernel,
        out_shape=[pltpu.VMEM(a.shape, a.dtype) for a in inputs]
        + [pltpu.VMEM((own, width), BF)] * 2
        + [pltpu.VMEM((2 * cols, width), BF)]
        + [pltpu.VMEM((3 * cols, width), BF)] * 2,
        in_specs=[pl.BlockSpec(memory_space=pl.ANY)] * len(inputs),
        scratch_shapes=[pltpu.SemaphoreType.DMA((len(inputs),))],
        compiler_params=VMEM_LIMIT,
    )(*[pltpu.with_memory_space_constraint(a, pltpu.MemorySpace.HBM) for a in inputs])
    from_next = lax.ppermute(up, "rows", [(i + 1, i) for i in range(NZ - 1)])
    from_prev = lax.ppermute(down, "rows", [(i, i + 1) for i in range(NZ - 1)])

    devices = NX * NY * NC
    conv_rows, expand_rows = width // devices, chans // devices
    shard_rows = conv_rows * taps // width + expand_rows
    part = (4, HX * HY * shard_rows, width)
    conv_part, expand_part, two_in, gtwo_in = call(
        inner_kernel,
        [pltpu.VMEM((width, taps), F32), pltpu.VMEM((chans, width), F32), pltpu.VMEM((own - cols, width), BF), pltpu.VMEM((own, width), BF)],
        halting, hidden, back, from_next, upstream, expand_in, weight_conv,
        scratch=[pltpu.VMEM((own, taps), BF)],
    )
    keep, send, two, gtwo = call(
        outer_kernel,
        [pltpu.VMEM(part, BF), pltpu.VMEM(part, BF), pltpu.VMEM((cols, width), BF), pltpu.VMEM((2 * cols, width), BF)],
        halting, hidden, back, from_prev, upstream, weight_conv, conv_part, expand_part,
        scratch=[pltpu.VMEM((2 * cols, taps), BF)],
    )

    got = lax.ppermute(send, "core", [(0, 1), (1, 0)])
    out, grad_in, done = call(
        functools.partial(leave_kernel, cols=cols),
        [jax.ShapeDtypeStruct((own, chans), BF)] * 2 + [pltpu.VMEM((8, 128), F32)],
        flat_in, upstream, two_in, two, gtwo_in, gtwo, sign, reduce_in, weight_conv, expand_in,
        scratch=[pltpu.VMEM((own, taps), BF), pltpu.VMEM((taps, width), BF)],
    )
    (total,) = call(core_kernel, [pltpu.VMEM(part, BF)], keep, got, done)
    got = lax.all_to_all(total, AXES, 0, 0, axis_index_groups=near_groups(), tiled=True)
    shard = (conv_rows, shard_rows // conv_rows * width // 2)
    (total,) = call(
        functools.partial(near_kernel, taps=taps // width), [pltpu.VMEM((2 * HX * HY,) + shard, BF)], got
    )
    got = lax.all_to_all(total, AXES, 0, 0, axis_index_groups=far_groups(), tiled=True)
    (total,) = call(plane_kernel, [pltpu.VMEM((NZ,) + shard, BF)], got)
    got = lax.all_to_all(total, "rows", 0, 0, tiled=True)
    grad_conv, grad_expand = call(
        rows_kernel,
        [jax.ShapeDtypeStruct((conv_rows, taps), F32), jax.ShapeDtypeStruct((expand_rows, width), F32)],
        got,
    )
    return (out.reshape(features.shape), grad_in.reshape(features.shape), grad_conv, grad_expand)


def solution(mesh):
    mesh = Mesh(mesh.devices.reshape(SIZES), AXES)
    whole = P(DP, "rows", None, None)
    in_specs = (whole, P(DP, "rows", None), whole, P(), P(), P())
    out_specs = (whole, whole, P(DP, None), P(DP, None))
    return jax.shard_map(local, mesh=mesh, in_specs=in_specs, out_specs=out_specs, check_vma=False)
```
